32 devices in a mesh: blk: 16 (over z, y, core), head: 2 (over x).
Axes of the slice: x: 2, y: 2, z: 4, core: 2. Of those that a mesh axis runs over, the one named last changes fastest.
Arguments:
- queries: bfloat16 [1024, 3584], P('blk', 'head'), may hold values from -64 to 64
- new_keys: bfloat16 [1024, 3584], P('blk', 'head'), may hold values from -6 to 6
- new_values: bfloat16 [1024, 3584], P('blk', 'head'), may hold values from -6 to 6
- key_cache: bfloat16 [128, 128, 3584], P('blk', None, 'head'), may hold values from -6 to 6
- value_cache: bfloat16 [128, 128, 3584], P('blk', None, 'head'), may hold values from -6 to 6
- out_weight: bfloat16 [3584, 3584], P('head'), may hold values from -0.09375 to 0.09375
- cache_len: int32 [1], replicated, may hold values from 1 to 16384, as said below
- page_table: int32 [128], replicated, may hold values from 0 to 127, each once
- block_perm: int32 [16], replicated, may hold values from 0 to 15, each once
Outputs:
- projected: bfloat16 [1024, 3584], P('blk', 'head')
The draws below stay inside these ranges and needn't reach their ends.
Inputs may be any that keep to these rules, and one draw needn't show every extreme that they name: `cache_len`: some request has exactly 16384 cached tokens. `page_table`: each global page appears once. `block_perm`: each query block appears once.
All inputs are finite; a program needn't handle non-finite values.
Results may differ from the reference program's by a relative error of at most 0.015.
Values may be sent and summed in bfloat16 or wider, within the bound.
A program may use at most 128 MiB of HBM per device.

```python
import math
import jax
import jax.numpy as jnp
from jax import lax

HEADS = 16
HD = 224
D_OUT = 3584
PAGE = 128
NEW = 1024
TOK_DEV = 64
TOKENS = 1024
REQS = 1
NPAGES = 128
LMAX = 16384
MAXP = 128
N_BLK = 16


def draw_queries(key, part):
    base_key = jax.random.fold_in(key, 1)
    drawn = jnp.clip(jax.random.normal(base_key, (TOKENS, HEADS * HD), jnp.float32), -6.0, 6.0)
    return drawn.astype(jnp.bfloat16)


def draw_key_cache(key, part):
    array_shape = (NPAGES, PAGE, HEADS * HD)
    base_key = jax.random.fold_in(key, 5)
    drawn = jnp.clip(jax.random.normal(base_key, array_shape, jnp.float32), -6.0, 6.0)
    return drawn.astype(jnp.bfloat16)


def draw_cache_len(key, part):
    lengths = jax.random.randint(jax.random.fold_in(key, 3), (REQS,), 1, LMAX + 1)
    longest = jax.random.randint(jax.random.fold_in(key, 4), (), 0, REQS)
    return jnp.where(jnp.arange(REQS) == longest, LMAX, lengths).astype(jnp.int32)


def block_levels(stream_key, shape, split, smallest, largest):
    gain, own = 1.0, jax.random.fold_in(stream_key, 6)
    for position, blocks in split:
        draws = jnp.exp(jax.random.uniform(jax.random.fold_in(own, position), (blocks,), jnp.float32, smallest / len(split), largest / len(split)))
        gain = gain * jnp.repeat(draws, shape[position] // blocks).reshape([-1 if axis == position else 1 for axis in range(len(shape))])
    return gain


def bell_draw(own_key, shape, spread, bound, cuts=(), kind=jnp.bfloat16):
    values = jax.random.normal(own_key, shape, jnp.float32) * spread
    if len(cuts) > 0:
        values = block_levels(own_key, shape, cuts, -0.22, 0.18) * values
    return jnp.clip(values, min=-bound, max=bound).astype(kind)


def setup_inputs(seed: int = 0) -> dict:
    streams_of = jax.random.split(jax.random.key(seed), 10)
    return {
        "queries": draw_queries(jax.random.fold_in(streams_of[9], 71), 0),
        "new_keys": bell_draw(streams_of[1], (TOKENS, HEADS * HD), 1.0, 6.0, ((0, 16), (1, 2))),
        "new_values": bell_draw(streams_of[2], (TOKENS, HEADS * HD), 1.0, 6.0, ((0, 16), (1, 2))),
        "key_cache": draw_key_cache(jax.random.fold_in(streams_of[9], 71), 0),
        "value_cache": bell_draw(streams_of[4], (NPAGES, PAGE, HEADS * HD), 1.0, 6.0, ((0, 16), (2, 2))),
        "out_weight": bell_draw(streams_of[5], (HEADS * HD, D_OUT), (HEADS * HD) ** -0.5, 0.09375, ((0, 2),)),
        "cache_len": draw_cache_len(jax.random.fold_in(streams_of[9], 71), 0),
        "page_table": jax.random.permutation(streams_of[7], NPAGES).astype(jnp.int32),
        "block_perm": jax.random.permutation(streams_of[8], N_BLK).astype(jnp.int32),
    }


def reference(queries, new_keys, new_values, key_cache, value_cache, out_weight, cache_len, page_table, block_perm):
    row_width = HEADS * HD
    block_ids = jnp.arange(N_BLK, dtype=jnp.int32)
    inverse = jnp.zeros((N_BLK,), jnp.int32).at[block_perm].set(block_ids)

    def to_global(dealt):
        return dealt.reshape(N_BLK, TOK_DEV, row_width)[inverse].reshape(REQS, NEW, row_width)
    query_all = to_global(queries)
    key_new = to_global(new_keys)
    value_new = to_global(new_values)
    page_grid = page_table.reshape(REQS, MAXP)
    score_scale = 1.0 / math.sqrt(HD)

    def one_request(request):
        page_rows = page_grid[request]
        key_rows = jnp.concatenate([key_cache[page_rows].reshape(LMAX, row_width), key_new[request]], axis=0)
        value_rows = jnp.concatenate([value_cache[page_rows].reshape(LMAX, row_width), value_new[request]], axis=0)
        positions = jnp.arange(LMAX + NEW, dtype=jnp.int32)[None, :]
        new_pos = jnp.arange(NEW, dtype=jnp.int32)[:, None]
        visible = jnp.where(positions < LMAX, positions < cache_len[request], positions - LMAX <= new_pos)
        query_rows = query_all[request]

        def one_head(head_index):
            start = head_index * HD
            q_part = lax.dynamic_slice_in_dim(query_rows, start, HD, 1)
            k_part = lax.dynamic_slice_in_dim(key_rows, start, HD, 1)
            v_part = lax.dynamic_slice_in_dim(value_rows, start, HD, 1)
            scores = jnp.dot(q_part, k_part.T, preferred_element_type=jnp.float32) * score_scale
            scores = jnp.where(visible, scores, -1e+30)
            row_top = lax.optimization_barrier(jnp.max(scores, axis=1, keepdims=True))
            weights = jnp.where(visible, jnp.exp(scores - row_top), 0.0)
            rounded = lax.optimization_barrier(weights.astype(jnp.bfloat16))
            total = lax.optimization_barrier(jnp.sum(rounded.astype(jnp.float32), axis=1, keepdims=True))
            numer = jnp.dot(rounded, v_part, preferred_element_type=jnp.float32)
            return numer / total
        head_outs = lax.map(one_head, jnp.arange(HEADS, dtype=jnp.int32))
        return jnp.transpose(head_outs, (1, 0, 2)).reshape(NEW, row_width)
    attended = lax.map(one_request, jnp.arange(REQS, dtype=jnp.int32))
    dealt = attended.reshape(N_BLK, TOK_DEV, row_width)[block_perm].reshape(N_BLK * TOK_DEV, row_width)
    mixed = dealt.astype(jnp.bfloat16)
    return jnp.dot(mixed, out_weight, preferred_element_type=jnp.float32).astype(jnp.bfloat16)
```

```python
import math

import jax
import jax.numpy as jnp
from jax import lax
from jax.experimental import pallas as pl
from jax.experimental.pallas import tpu as pltpu
from jax.sharding import PartitionSpec as P

HD = 224
PAGE = 128
P_DEV = 8
NEW = 1024
TOK_DEV = 64
MAXP = 128


def block_partial(query_rows, key_rows, value_rows, visible):
    head_count = query_rows.shape[1] // HD
    query_heads = query_rows.reshape(query_rows.shape[0], head_count, HD)
    key_heads = key_rows.reshape(key_rows.shape[0], head_count, HD)
    value_heads = value_rows.reshape(value_rows.shape[0], head_count, HD)
    scores = jnp.einsum(
        "qhd,khd->hqk", query_heads, key_heads, preferred_element_type=jnp.float32
    ) * (1.0 / math.sqrt(HD))
    scores = jnp.where(visible[None], scores, -1e30)
    row_top = jnp.max(scores, axis=2)
    weights = jnp.where(visible[None], jnp.exp(scores - row_top[:, :, None]), 0.0).astype(
        jnp.bfloat16
    )
    row_sum = jnp.sum(weights.astype(jnp.float32), axis=2)
    numerators = jnp.einsum(
        "hqk,khd->qhd", weights, value_heads, preferred_element_type=jnp.float32
    )
    return (row_top.T, row_sum.T, numerators)


def absorb(carry_state, request, partial_value):
    numer_all, top_all, sum_all = carry_state
    part_top, part_sum, part_numer = partial_value
    old_top = lax.dynamic_index_in_dim(top_all, request, 0, keepdims=False)
    old_sum = lax.dynamic_index_in_dim(sum_all, request, 0, keepdims=False)
    old_numer = lax.dynamic_index_in_dim(numer_all, request, 0, keepdims=False)
    new_top = jnp.maximum(old_top, part_top)
    old_factor = jnp.exp(old_top - new_top)
    part_factor = jnp.exp(part_top - new_top)
    merged_sum = old_factor * old_sum + part_factor * part_sum
    merged_numer = old_numer * old_factor[:, :, None] + part_numer * part_factor[:, :, None]
    return (
        lax.dynamic_update_index_in_dim(numer_all, merged_numer, request, 0),
        lax.dynamic_update_index_in_dim(top_all, new_top, request, 0),
        lax.dynamic_update_index_in_dim(sum_all, merged_sum, request, 0),
    )


def shards(
    queries,
    new_keys,
    new_values,
    key_cache,
    value_cache,
    out_weight,
    cache_len,
    page_table,
    block_perm,
):
    row_width = queries.shape[1]
    head_count = row_width // HD
    blk_count = lax.axis_size("blk")
    my_index = lax.axis_index("blk")
    req_count = cache_len.shape[0]
    blocks_per_req = NEW // TOK_DEV
    gathered = lax.all_gather(queries, "blk", axis=0, tiled=True)
    block_ids = jnp.arange(blk_count, dtype=jnp.int32)
    inverse = jnp.zeros((blk_count,), jnp.int32).at[block_perm].set(block_ids)
    query_all = gathered.reshape(blk_count, TOK_DEV, row_width)[inverse].reshape(
        req_count, NEW, row_width
    )
    global_ids = my_index * P_DEV + jnp.arange(P_DEV, dtype=jnp.int32)
    table_ids = jnp.arange(page_table.shape[0], dtype=jnp.int32)
    match_rows = page_table[None, :] == global_ids[:, None]
    logical = jnp.sum(jnp.where(match_rows, table_ids[None, :], 0), axis=1)
    page_req = logical // MAXP
    page_pos = logical % MAXP
    page_fill = jnp.clip(cache_len[page_req] - page_pos * PAGE, 0, PAGE)
    slot_ids = jnp.arange(PAGE, dtype=jnp.int32)
    start_state = (
        jnp.zeros((req_count, NEW, head_count, HD), jnp.float32),
        jnp.full((req_count, NEW, head_count), -1e30, jnp.float32),
        jnp.zeros((req_count, NEW, head_count), jnp.float32),
    )

    def page_work(slot_index, carry_state):
        request = page_req[slot_index]
        query_rows = lax.dynamic_index_in_dim(query_all, request, 0, keepdims=False)
        key_rows = lax.dynamic_index_in_dim(key_cache, slot_index, 0, keepdims=False)
        value_rows = lax.dynamic_index_in_dim(value_cache, slot_index, 0, keepdims=False)
        visible = jnp.broadcast_to((slot_ids < page_fill[slot_index])[None, :], (NEW, PAGE))
        return absorb(
            carry_state, request, block_partial(query_rows, key_rows, value_rows, visible)
        )

    def page_step(slot_index, carry_state):
        return page_work(slot_index, carry_state)

    carry_state = lax.fori_loop(0, P_DEV, page_step, start_state)
    my_block = block_perm[my_index]
    my_request = my_block // blocks_per_req
    my_offset = my_block % blocks_per_req * TOK_DEV
    new_pos = jnp.arange(NEW, dtype=jnp.int32)[:, None]
    key_pos = my_offset + jnp.arange(TOK_DEV, dtype=jnp.int32)[None, :]
    own_rows = lax.dynamic_index_in_dim(query_all, my_request, 0, keepdims=False)
    carry_state = absorb(
        carry_state, my_request, block_partial(own_rows, new_keys, new_values, new_pos >= key_pos)
    )
    numer_all, top_all, sum_all = carry_state
    send_numer = numer_all.reshape(blk_count, TOK_DEV, row_width)[block_perm]
    send_top = top_all.reshape(blk_count, TOK_DEV, head_count)[block_perm]
    send_sum = sum_all.reshape(blk_count, TOK_DEV, head_count)[block_perm]
    recv_numer, recv_top, recv_sum = (
        lax.all_to_all(send_numer, "blk", split_axis=0, concat_axis=0, tiled=True),
        lax.all_to_all(send_top, "blk", split_axis=0, concat_axis=0, tiled=True),
        lax.all_to_all(send_sum, "blk", split_axis=0, concat_axis=0, tiled=True),
    )
    best_top = jnp.max(recv_top, axis=0)
    factor = jnp.exp(recv_top - best_top[None])
    total_sum = jnp.sum(recv_sum * factor, axis=0)
    total_numer = jnp.sum(
        recv_numer.reshape(blk_count, TOK_DEV, head_count, HD) * factor[..., None], axis=0
    )
    mixed = (total_numer / total_sum[:, :, None]).reshape(TOK_DEV, row_width).astype(jnp.bfloat16)
    head_term = jnp.dot(mixed, out_weight, preferred_element_type=jnp.float32)
    return lax.psum_scatter(head_term, "head", scatter_dimension=1, tiled=True).astype(jnp.bfloat16)


MESH = pl.DeviceIdType.MESH
Z, Y, CORES, XS = 4, 2, 2, 2
HEADS_CORE = 4
GROUP = HEADS_CORE * HD
CACHED = CORES * P_DEV * PAGE
FRESH = CORES * TOK_DEV
KEYS = CACHED + FRESH
QCHIP = CORES * TOK_DEV
QW = Y * QCHIP
VROWS = HD + 16
COLS = 1792
LOG2_SCALE = math.log2(math.e) / math.sqrt(HD)


def fits_fused(mesh):
    return dict(mesh.shape) == {"blk": Z * Y * CORES, "head": XS}


def fused_kernel(
    perm, q_hbm, nk_hbm, nv_hbm, kc_hbm, vc_hbm, w_hbm, out_ref,
    q_stage, nk_stage, nv_stage, k_stage, v_stage, w_all,
    q_t, k_heads, v_t, scores, probs,
    part, part_16, part_stat, y_part, y_stat,
    z_src, z_src_stat, z_part, z_stat,
    acc, c_part, x_src, x_part,
    local_sem, core_send, core_recv, gz_send, gz_recv, gy_send, gy_recv,
    ry_send, ry_recv, rz_send, rz_recv, o_send, o_recv,
):
    me = lax.axis_index("blk")
    x = lax.axis_index("head")
    core = me % CORES
    y = (me // CORES) % Y
    z = me // (CORES * Y)

    def blk_of(zz, yy, cc):
        return (zz * Y + yy) * CORES + cc

    sibling = (blk_of(z, y, 1 - core), x)
    y_peer = (blk_of(z, 1 - y, core), x)
    x_peer = (me, 1 - x)
    z_to = [None] + [(blk_of((z + d) % Z, y, core), x) for d in range(1, Z)]
    barrier = pltpu.get_barrier_semaphore()
    for peer in [sibling, y_peer, x_peer] + z_to[1:]:
        pl.semaphore_signal(barrier, inc=1, device_id=peer, device_id_type=MESH)
    pl.semaphore_wait(barrier, Z + 2)

    mine = pl.ds(pl.multiple_of(core * GROUP, 128), GROUP)
    theirs = pl.ds(pl.multiple_of((1 - core) * GROUP, 128), GROUP)
    staged = [
        (q_hbm, q_stage), (kc_hbm, k_stage), (vc_hbm, v_stage),
        (nk_hbm, nk_stage), (nv_hbm, nv_stage),
    ]
    local_copies, core_copies = [], []
    for i, (src, dst) in enumerate(staged):
        lead = (slice(None),) * (len(src.shape) - 1)
        copy = pltpu.make_async_copy(src.at[lead + (mine,)], dst.at[core], local_sem.at[i])
        copy.start()
        local_copies.append(copy)
        copy = pltpu.make_async_remote_copy(
            src_ref=src.at[lead + (theirs,)], dst_ref=dst.at[core],
            send_sem=core_send.at[i], recv_sem=core_recv.at[i],
            device_id=sibling, device_id_type=MESH)
        copy.start()
        core_copies.append(copy)
    w_copy = pltpu.make_async_copy(
        w_hbm.at[pl.ds(pl.multiple_of(core * GROUP, 128), GROUP), :], w_all, local_sem.at[5])
    w_copy.start()

    pending = list(core_copies)

    def remote(src, dst, send_sem, recv_sem, peer):
        copy = pltpu.make_async_remote_copy(
            src_ref=src, dst_ref=dst, send_sem=send_sem, recv_sem=recv_sem,
            device_id=peer, device_id_type=MESH)
        copy.start()
        return copy

    local_copies[0].wait()
    core_copies[0].wait_recv()
    q_rows = jnp.concatenate([q_stage[0], q_stage[1]], axis=0).astype(jnp.float32)
    q_cols = q_rows.T.astype(jnp.bfloat16)
    for h in range(HEADS_CORE):
        q_t[h, z, y] = q_cols[h * HD:(h + 1) * HD]

    gather_z, gather_y, red_y, red_z = {}, {}, {}, {}
    for h in range(HEADS_CORE):
        block = q_t.at[h, z, y]
        gather_y[h, 0] = remote(block, block, gy_send.at[h, 0], gy_recv.at[h, 0], y_peer)
        for d in range(1, Z):
            gather_z[h, d] = remote(block, block, gz_send.at[h, d], gz_recv.at[h, d], z_to[d])

    def forward(h):
        for d in range(1, Z):
            gather_z[h, d].wait_recv()
            block = q_t.at[h, (z + Z - d) % Z, y]
            gather_y[h, d] = remote(block, block, gy_send.at[h, d], gy_recv.at[h, d], y_peer)

    def place_keys(rows, at, count):
        wide = rows.astype(jnp.float32)
        for h in range(HEADS_CORE):
            k_heads[h, pl.ds(at, count), :] = wide[:, h * HD:(h + 1) * HD].astype(jnp.bfloat16)

    def place_values(rows, at):
        tall = rows.astype(jnp.float32).T.astype(jnp.bfloat16)
        for h in range(HEADS_CORE):
            v_t[h, pl.ds(0, HD), pl.ds(at, PAGE)] = tall[h * HD:(h + 1) * HD]

    v_t[:, pl.ds(HD, VROWS - HD), :] = jnp.ones((HEADS_CORE, VROWS - HD, KEYS), jnp.bfloat16)

    local_copies[1].wait()
    core_copies[1].wait_recv()

    @pl.loop(0, CORES * P_DEV)
    def _(page):
        at = pl.multiple_of(page * PAGE, PAGE)
        place_keys(k_stage[page // P_DEV, page % P_DEV], at, PAGE)

    forward(0)
    local_copies[2].wait()
    core_copies[2].wait_recv()

    @pl.loop(0, CORES * P_DEV)
    def _(page):
        at = pl.multiple_of(page * PAGE, PAGE)
        place_values(v_stage[page // P_DEV, page % P_DEV], at)

    local_copies[3].wait()
    core_copies[3].wait_recv()
    local_copies[4].wait()
    core_copies[4].wait_recv()
    place_keys(jnp.concatenate([nk_stage[0], nk_stage[1]], axis=0), CACHED, FRESH)
    place_values(jnp.concatenate([nv_stage[0], nv_stage[1]], axis=0), CACHED)

    row = lax.broadcasted_iota(jnp.int32, (FRESH, QW), 0)
    lane = lax.broadcasted_iota(jnp.int32, (FRESH, QW), 1)
    key_pos = jnp.where(
        row < TOK_DEV, perm[blk_of(z, y, 0)], perm[blk_of(z, y, 1)]) * TOK_DEV + row % TOK_DEV
    tile_row = lax.broadcasted_iota(jnp.int32, (8, QCHIP), 0)

    def attend(h):
        @pl.loop(0, Z)
        def _(g):
            queries = jnp.concatenate([q_t[h, g, 0], q_t[h, g, 1]], axis=1)
            query_blk = jnp.zeros((FRESH, QW), jnp.int32)
            for j in range(Y * CORES):
                query_blk = jnp.where(lane // TOK_DEV == j, perm[g * Y * CORES + j], query_blk)
            seen = query_blk * TOK_DEV + lane % TOK_DEV >= key_pos
            fresh = jnp.dot(
                k_heads[h, pl.ds(CACHED, FRESH), :], queries, preferred_element_type=jnp.float32)
            fresh = jnp.where(seen, fresh, -1e30)
            scores[pl.ds(CACHED, FRESH), :] = fresh
            top = jnp.max(fresh.reshape(FRESH // 8, 8, QW), axis=0)
            for i in range(CACHED // 256):
                tile = jnp.dot(
                    k_heads[h, pl.ds(i * 256, 256), :], queries,
                    preferred_element_type=jnp.float32)
                scores[pl.ds(i * 256, 256), :] = tile
                top = jnp.maximum(top, jnp.max(tile.reshape(32, 8, QW), axis=0))
            top = jnp.max(top, axis=0, keepdims=True) * LOG2_SCALE
            for i in range(KEYS // 128):
                tile = scores[pl.ds(i * 128, 128), :]
                probs[pl.ds(i * 128, 128), :] = jnp.exp2(tile * LOG2_SCALE - top).astype(
                    jnp.bfloat16)
            numer = jnp.dot(v_t[h], probs[...], preferred_element_type=jnp.float32)
            for j in range(Y):
                cols = slice(j * QCHIP, (j + 1) * QCHIP)
                part[h, j, g] = numer[:HD, cols]
                part_16[h, j, g] = numer[:HD, cols].astype(jnp.bfloat16)
                part_stat[h, j, g] = jnp.where(
                    tile_row == 0, top[:, cols], numer[HD:HD + 1, cols])

    def send_y(h):
        red_y[h] = (
            remote(part_16.at[h, 1 - y], y_part.at[h], ry_send.at[h, 0], ry_recv.at[h, 0], y_peer),
            remote(part_stat.at[h, 1 - y], y_stat.at[h], ry_send.at[h, 1], ry_recv.at[h, 1], y_peer),
        )

    def merge_y(h):
        for copy in red_y[h]:
            copy.wait_recv()

        @pl.loop(0, Z)
        def _(g):
            own, other = part_stat[h, y, g], y_stat[h, g]
            top = jnp.maximum(own[0:1], other[0:1])
            own_factor, other_factor = jnp.exp2(own[0:1] - top), jnp.exp2(other[0:1] - top)
            total = own[1:2] * own_factor + other[1:2] * other_factor
            numer = part[h, y, g] * own_factor + y_part[h, g].astype(jnp.float32) * other_factor
            z_src[h, g] = numer.astype(jnp.bfloat16)
            z_src_stat[h, g] = jnp.where(tile_row == 0, top, total)

        for d in range(1, Z):
            to = (z + d) % Z
            red_z[h, d] = (
                remote(z_src.at[h, to], z_part.at[h, d], rz_send.at[h, d, 0], rz_recv.at[h, d, 0], z_to[d]),
                remote(z_src_stat.at[h, to], z_stat.at[h, d], rz_send.at[h, d, 1], rz_recv.at[h, d, 1], z_to[d]),
            )

    def finish(h):
        for d in range(1, Z):
            for copy in red_z[h, d]:
                copy.wait_recv()
        stats = [z_src_stat[h, z]] + [z_stat[h, d] for d in range(1, Z)]
        numers = [z_src[h, z]] + [z_part[h, d] for d in range(1, Z)]
        top = stats[0][0:1]
        for stat in stats[1:]:
            top = jnp.maximum(top, stat[0:1])
        total = jnp.zeros((1, QCHIP), jnp.float32)
        numer = jnp.zeros((HD, QCHIP), jnp.float32)
        for stat, term in zip(stats, numers):
            factor = jnp.exp2(stat[0:1] - top)
            total = total + stat[1:2] * factor
            numer = numer + term.astype(jnp.float32) * factor
        mixed = (numer / total).T.astype(jnp.bfloat16)
        for half in range(XS):
            for i in range(COLS // 256):
                cols = pl.ds(i * 256, 256)
                term = jnp.dot(
                    mixed, w_all[pl.ds(h * HD, HD), pl.ds(half * COLS + i * 256, 256)],
                    preferred_element_type=jnp.float32)
                for c in range(CORES):
                    rows = term[c * TOK_DEV:(c + 1) * TOK_DEV]
                    if h == 0:
                        acc[half, c, :, cols] = rows
                    else:
                        acc[half, c, :, cols] += rows

    for h in range(HEADS_CORE):
        if h + 1 < HEADS_CORE:
            forward(h + 1)
        for d in range(Z):
            gather_y[h, d].wait_recv()
        attend(h)
        send_y(h)
        if h == 0:
            w_copy.wait()
        if h >= 1:
            merge_y(h - 1)
        if h >= 2:
            finish(h - 2)
    merge_y(HEADS_CORE - 1)
    finish(HEADS_CORE - 2)
    finish(HEADS_CORE - 1)

    away = remote(acc.at[1 - x, 1 - core], c_part.at[0], o_send.at[0], o_recv.at[0], sibling)
    home = remote(acc.at[x, 1 - core], c_part.at[1], o_send.at[1], o_recv.at[1], sibling)
    away.wait_recv()
    x_src[...] = (acc[1 - x, core] + c_part[0]).astype(jnp.bfloat16)
    across = remote(x_src, x_part, o_send.at[2], o_recv.at[2], x_peer)
    home.wait_recv()
    c_part[1] = acc[x, core] + c_part[1]
    across.wait_recv()
    out_ref[...] = (c_part[1] + x_part[...].astype(jnp.float32)).astype(jnp.bfloat16)

    pending += [away, home, across]
    pending += list(gather_z.values()) + list(gather_y.values())
    for copies in list(red_y.values()) + list(red_z.values()):
        pending += list(copies)
    for copy in pending:
        copy.wait_send()


def fused_shards(
    queries, new_keys, new_values, key_cache, value_cache, out_weight,
    cache_len, page_table, block_perm,
):
    bf16, f32 = jnp.bfloat16, jnp.float32
    vmem, dma = pltpu.VMEM, pltpu.SemaphoreType.DMA
    hc = HEADS_CORE
    block = (HD, QCHIP)
    stat = (8, QCHIP)
    scratch = [
        vmem((CORES, TOK_DEV, GROUP), bf16),
        vmem((CORES, TOK_DEV, GROUP), bf16),
        vmem((CORES, TOK_DEV, GROUP), bf16),
        vmem((CORES, P_DEV, PAGE, GROUP), bf16),
        vmem((CORES, P_DEV, PAGE, GROUP), bf16),
        vmem((GROUP, XS * COLS), bf16),
        vmem((hc, Z, Y) + block, bf16),
        vmem((hc, KEYS, HD), bf16),
        vmem((hc, VROWS, KEYS), bf16),
        vmem((KEYS, QW), f32),
        vmem((KEYS, QW), bf16),
        vmem((hc, Y, Z) + block, f32),
        vmem((hc, Y, Z) + block, bf16),
        vmem((hc, Y, Z) + stat, f32),
        vmem((hc, Z) + block, bf16),
        vmem((hc, Z) + stat, f32),
        vmem((hc, Z) + block, bf16),
        vmem((hc, Z) + stat, f32),
        vmem((hc, Z) + block, bf16),
        vmem((hc, Z) + stat, f32),
        vmem((XS, CORES, TOK_DEV, COLS), f32),
        vmem((2, TOK_DEV, COLS), f32),
        vmem((TOK_DEV, COLS), bf16),
        vmem((TOK_DEV, COLS), bf16),
        dma((6,)), dma((5,)), dma((5,)),
        dma((hc, Z)), dma((hc, Z)), dma((hc, Z)), dma((hc, Z)),
        dma((hc, 2)), dma((hc, 2)), dma((hc, Z, 2)), dma((hc, Z, 2)),
        dma((3,)), dma((3,)),
    ]
    flops = 4 * hc * Z * QW * KEYS * HD + 2 * QCHIP * GROUP * XS * COLS
    return pl.pallas_call(
        fused_kernel,
        out_shape=jax.ShapeDtypeStruct((TOK_DEV, COLS), bf16),
        in_specs=[pl.BlockSpec(memory_space=pltpu.SMEM)] + [pl.BlockSpec(memory_space=pl.ANY)] * 6,
        out_specs=pl.BlockSpec(memory_space=pltpu.VMEM),
        scratch_shapes=scratch,
        compiler_params=pltpu.CompilerParams(
            collective_id=0, has_side_effects=True, vmem_limit_bytes=56 * 1024 * 1024),
        cost_estimate=pl.CostEstimate(
            flops=flops, bytes_accessed=14 * 1024 * 1024, transcendentals=hc * Z * QW * KEYS),
    )(block_perm, queries, new_keys, new_values, key_cache, value_cache, out_weight)


def solution(mesh):
    in_specs = (
        P("blk", "head"),
        P("blk", "head"),
        P("blk", "head"),
        P("blk", None, "head"),
        P("blk", None, "head"),
        P("head", None),
        P(),
        P(),
        P(),
    )
    out_specs = P("blk", "head")
    local = fused_shards if fits_fused(mesh) else shards
    return jax.shard_map(local, mesh=mesh, in_specs=in_specs, out_specs=out_specs, check_vma=False)
```

```python
import math

import jax
import jax.numpy as jnp
from jax import lax
from jax.experimental import pallas as pl
from jax.experimental.pallas import tpu as pltpu
from jax.sharding import PartitionSpec as P

HD = 224
PAGE = 128
P_DEV = 8
NEW = 1024
TOK_DEV = 64
MAXP = 128


def block_partial(query_rows, key_rows, value_rows, visible):
    head_count = query_rows.shape[1] // HD
    query_heads = query_rows.reshape(query_rows.shape[0], head_count, HD)
    key_heads = key_rows.reshape(key_rows.shape[0], head_count, HD)
    value_heads = value_rows.reshape(value_rows.shape[0], head_count, HD)
    scores = jnp.einsum(
        "qhd,khd->hqk", query_heads, key_heads, preferred_element_type=jnp.float32
    ) * (1.0 / math.sqrt(HD))
    scores = jnp.where(visible[None], scores, -1e30)
    row_top = jnp.max(scores, axis=2)
    weights = jnp.where(visible[None], jnp.exp(scores - row_top[:, :, None]), 0.0).astype(
        jnp.bfloat16
    )
    row_sum = jnp.sum(weights.astype(jnp.float32), axis=2)
    numerators = jnp.einsum(
        "hqk,khd->qhd", weights, value_heads, preferred_element_type=jnp.float32
    )
    return (row_top.T, row_sum.T, numerators)


def absorb(carry_state, request, partial_value):
    numer_all, top_all, sum_all = carry_state
    part_top, part_sum, part_numer = partial_value
    old_top = lax.dynamic_index_in_dim(top_all, request, 0, keepdims=False)
    old_sum = lax.dynamic_index_in_dim(sum_all, request, 0, keepdims=False)
    old_numer = lax.dynamic_index_in_dim(numer_all, request, 0, keepdims=False)
    new_top = jnp.maximum(old_top, part_top)
    old_factor = jnp.exp(old_top - new_top)
    part_factor = jnp.exp(part_top - new_top)
    merged_sum = old_factor * old_sum + part_factor * part_sum
    merged_numer = old_numer * old_factor[:, :, None] + part_numer * part_factor[:, :, None]
    return (
        lax.dynamic_update_index_in_dim(numer_all, merged_numer, request, 0),
        lax.dynamic_update_index_in_dim(top_all, new_top, request, 0),
        lax.dynamic_update_index_in_dim(sum_all, merged_sum, request, 0),
    )


def shards(
    queries,
    new_keys,
    new_values,
    key_cache,
    value_cache,
    out_weight,
    cache_len,
    page_table,
    block_perm,
):
    row_width = queries.shape[1]
    head_count = row_width // HD
    blk_count = lax.axis_size("blk")
    my_index = lax.axis_index("blk")
    req_count = cache_len.shape[0]
    blocks_per_req = NEW // TOK_DEV
    gathered = lax.all_gather(queries, "blk", axis=0, tiled=True)
    block_ids = jnp.arange(blk_count, dtype=jnp.int32)
    inverse = jnp.zeros((blk_count,), jnp.int32).at[block_perm].set(block_ids)
    query_all = gathered.reshape(blk_count, TOK_DEV, row_width)[inverse].reshape(
        req_count, NEW, row_width
    )
    global_ids = my_index * P_DEV + jnp.arange(P_DEV, dtype=jnp.int32)
    table_ids = jnp.arange(page_table.shape[0], dtype=jnp.int32)
    match_rows = page_table[None, :] == global_ids[:, None]
    logical = jnp.sum(jnp.where(match_rows, table_ids[None, :], 0), axis=1)
    page_req = logical // MAXP
    page_pos = logical % MAXP
    page_fill = jnp.clip(cache_len[page_req] - page_pos * PAGE, 0, PAGE)
    slot_ids = jnp.arange(PAGE, dtype=jnp.int32)
    start_state = (
        jnp.zeros((req_count, NEW, head_count, HD), jnp.float32),
        jnp.full((req_count, NEW, head_count), -1e30, jnp.float32),
        jnp.zeros((req_count, NEW, head_count), jnp.float32),
    )

    def page_work(slot_index, carry_state):
        request = page_req[slot_index]
        query_rows = lax.dynamic_index_in_dim(query_all, request, 0, keepdims=False)
        key_rows = lax.dynamic_index_in_dim(key_cache, slot_index, 0, keepdims=False)
        value_rows = lax.dynamic_index_in_dim(value_cache, slot_index, 0, keepdims=False)
        visible = jnp.broadcast_to((slot_ids < page_fill[slot_index])[None, :], (NEW, PAGE))
        return absorb(
            carry_state, request, block_partial(query_rows, key_rows, value_rows, visible)
        )

    def page_step(slot_index, carry_state):
        return page_work(slot_index, carry_state)

    carry_state = lax.fori_loop(0, P_DEV, page_step, start_state)
    my_block = block_perm[my_index]
    my_request = my_block // blocks_per_req
    my_offset = my_block % blocks_per_req * TOK_DEV
    new_pos = jnp.arange(NEW, dtype=jnp.int32)[:, None]
    key_pos = my_offset + jnp.arange(TOK_DEV, dtype=jnp.int32)[None, :]
    own_rows = lax.dynamic_index_in_dim(query_all, my_request, 0, keepdims=False)
    carry_state = absorb(
        carry_state, my_request, block_partial(own_rows, new_keys, new_values, new_pos >= key_pos)
    )
    numer_all, top_all, sum_all = carry_state
    send_numer = numer_all.reshape(blk_count, TOK_DEV, row_width)[block_perm]
    send_top = top_all.reshape(blk_count, TOK_DEV, head_count)[block_perm]
    send_sum = sum_all.reshape(blk_count, TOK_DEV, head_count)[block_perm]
    recv_numer, recv_top, recv_sum = (
        lax.all_to_all(send_numer, "blk", split_axis=0, concat_axis=0, tiled=True),
        lax.all_to_all(send_top, "blk", split_axis=0, concat_axis=0, tiled=True),
        lax.all_to_all(send_sum, "blk", split_axis=0, concat_axis=0, tiled=True),
    )
    best_top = jnp.max(recv_top, axis=0)
    factor = jnp.exp(recv_top - best_top[None])
    total_sum = jnp.sum(recv_sum * factor, axis=0)
    total_numer = jnp.sum(
        recv_numer.reshape(blk_count, TOK_DEV, head_count, HD) * factor[..., None], axis=0
    )
    mixed = (total_numer / total_sum[:, :, None]).reshape(TOK_DEV, row_width).astype(jnp.bfloat16)
    head_term = jnp.dot(mixed, out_weight, preferred_element_type=jnp.float32)
    return lax.psum_scatter(head_term, "head", scatter_dimension=1, tiled=True).astype(jnp.bfloat16)


MESH = pl.DeviceIdType.MESH
Z, Y, CORES, XS = 4, 2, 2, 2
HEADS_CORE = 4
GROUP = HEADS_CORE * HD
CACHED = CORES * P_DEV * PAGE
FRESH = CORES * TOK_DEV
KEYS = CACHED + FRESH
QCHIP = CORES * TOK_DEV
QW = Y * QCHIP
VROWS = HD + 16
COLS = 1792
CHUNK = COLS // 2
WINDOW = 384
UNITS = HEADS_CORE * Z
LAG = 2
LOG2_SCALE = math.log2(math.e) / math.sqrt(HD)


def fits_fused(mesh):
    return dict(mesh.shape) == {"blk": Z * Y * CORES, "head": XS}


def fused_kernel(
    perm, q_hbm, nk_hbm, nv_hbm, kc_hbm, vc_hbm, w_hbm, out_ref,
    q_stage, nk_stage, nv_stage, k_stage, v_stage, w_all,
    q_t, k_heads, v_t, scores_a, scores_b, probs_a, probs_b, tops,
    part, part_16, part_stat, y_part, y_stat,
    z_src, z_src_stat, z_part, z_stat,
    acc, c_part, x_src, x_part,
    local_sem, core_send, core_recv, gz_send, gz_recv, gy_send, gy_recv,
    ry_send, ry_recv, rz_send, rz_recv, o_send, o_recv,
):
    me = lax.axis_index("blk")
    x = lax.axis_index("head")
    core = me % CORES
    y = (me // CORES) % Y
    z = me // (CORES * Y)
    scores, probs = (scores_a, scores_b), (probs_a, probs_b)

    def blk_of(zz, yy, cc):
        return (zz * Y + yy) * CORES + cc

    sibling = (blk_of(z, y, 1 - core), x)
    y_peer = (blk_of(z, 1 - y, core), x)
    x_peer = (me, 1 - x)

    def z_to(d):
        return (blk_of((z + d) % Z, y, core), x)

    barrier = pltpu.get_barrier_semaphore()
    for peer in [sibling, y_peer, x_peer] + [z_to(d) for d in range(1, Z)]:
        pl.semaphore_signal(barrier, inc=1, device_id=peer, device_id_type=MESH)
    pl.semaphore_wait(barrier, Z + 2)

    def remote(src, dst, send_sem, recv_sem, peer):
        return pltpu.make_async_remote_copy(
            src_ref=src, dst_ref=dst, send_sem=send_sem, recv_sem=recv_sem,
            device_id=peer, device_id_type=MESH)

    mine = pl.ds(pl.multiple_of(core * GROUP, 128), GROUP)
    theirs = pl.ds(pl.multiple_of((1 - core) * GROUP, 128), GROUP)
    staged = [
        (q_hbm, q_stage), (kc_hbm, k_stage), (nk_hbm, nk_stage),
        (vc_hbm, v_stage), (nv_hbm, nv_stage),
    ]
    local_copies, core_copies = [], []
    for i, (src, dst) in enumerate(staged):
        lead = (slice(None),) * (len(src.shape) - 1)
        copy = remote(
            src.at[lead + (theirs,)], dst.at[core], core_send.at[i], core_recv.at[i], sibling)
        copy.start()
        core_copies.append(copy)
        copy = pltpu.make_async_copy(src.at[lead + (mine,)], dst.at[core], local_sem.at[i])
        copy.start()
        local_copies.append(copy)
    w_copy = pltpu.make_async_copy(
        w_hbm.at[pl.ds(pl.multiple_of(core * GROUP, 128), GROUP), :], w_all, local_sem.at[5])
    w_copy.start()

    def arrived(i):
        local_copies[i].wait()
        core_copies[i].wait_recv()

    def gather_z(h, d):
        block = q_t.at[h, z, y]
        return remote(block, block, gz_send.at[h, d], gz_recv.at[h, d], z_to(d))

    def gather_y(h, d):
        block = q_t.at[h, (z + Z - d) % Z, y]
        return remote(block, block, gy_send.at[h, d], gy_recv.at[h, d], y_peer)

    def forward(h, d):
        gather_z(h, d).wait_recv()
        gather_y(h, d).start()

    def reduce_y(h, g):
        return (
            remote(part_16.at[h, g, 1 - y], y_part.at[h, g],
                   ry_send.at[h, g, 0], ry_recv.at[h, g, 0], y_peer),
            remote(part_stat.at[h, g, 1 - y], y_stat.at[h, g],
                   ry_send.at[h, g, 1], ry_recv.at[h, g, 1], y_peer),
        )

    def reduce_z(h, d):
        to = (z + d) % Z
        return (
            remote(z_src.at[h, to], z_part.at[h, d],
                   rz_send.at[h, d, 0], rz_recv.at[h, d, 0], z_to(d)),
            remote(z_src_stat.at[h, to], z_stat.at[h, d],
                   rz_send.at[h, d, 1], rz_recv.at[h, d, 1], z_to(d)),
        )

    arrived(0)
    q_rows = jnp.concatenate([q_stage[0], q_stage[1]], axis=0).astype(jnp.float32)
    q_cols = q_rows.T.astype(jnp.bfloat16)
    for h in range(HEADS_CORE):
        q_t[h, z, y] = q_cols[h * HD:(h + 1) * HD]
    for h in range(HEADS_CORE):
        gather_y(h, 0).start()
        for d in range(1, Z):
            gather_z(h, d).start()

    v_t[:, pl.ds(HD, VROWS - HD), :] = jnp.ones((HEADS_CORE, VROWS - HD, KEYS), jnp.bfloat16)
    acc[...] = jnp.zeros(acc.shape, jnp.float32)

    def head_window(h):
        start = jnp.minimum(h * HD // 128 * 128, GROUP - WINDOW)
        return pl.ds(pl.multiple_of(start, 128), WINDOW), h * HD - start

    def prepare_keys(h):
        window, offset = head_window(h)
        pick = jnp.where(
            lax.broadcasted_iota(jnp.int32, (WINDOW, HD), 0)
            == lax.broadcasted_iota(jnp.int32, (WINDOW, HD), 1) + offset, 1.0, 0.0
        ).astype(jnp.bfloat16)

        def place(rows, at, count):
            k_heads[h, pl.ds(at, count), :] = jnp.dot(
                rows, pick, preferred_element_type=jnp.float32).astype(jnp.bfloat16)

        for c in range(CORES):
            for page in range(0, P_DEV, 2):
                rows = k_stage[c, pl.ds(page, 2), :, window].reshape(2 * PAGE, WINDOW)
                place(rows, (c * P_DEV + page) * PAGE, 2 * PAGE)
            place(nk_stage[c, :, window], CACHED + c * TOK_DEV, TOK_DEV)

    def prepare_values(h):
        window, offset = head_window(h)
        pick = jnp.where(
            lax.broadcasted_iota(jnp.int32, (HD, WINDOW), 1)
            == lax.broadcasted_iota(jnp.int32, (HD, WINDOW), 0) + offset, 1.0, 0.0
        ).astype(jnp.bfloat16)

        def place(rows, at, count):
            v_t[h, pl.ds(0, HD), pl.ds(at, count)] = lax.dot_general(
                pick, rows, (((1,), (1,)), ((), ())), preferred_element_type=jnp.float32
            ).astype(jnp.bfloat16)

        for c in range(CORES):
            for page in range(0, P_DEV, 2):
                rows = v_stage[c, pl.ds(page, 2), :, window].reshape(2 * PAGE, WINDOW)
                place(rows, (c * P_DEV + page) * PAGE, 2 * PAGE)
        place(jnp.concatenate([nv_stage[c, :, window] for c in range(CORES)], axis=0), CACHED, FRESH)

    row = lax.broadcasted_iota(jnp.int32, (FRESH, QW), 0)
    lane = lax.broadcasted_iota(jnp.int32, (FRESH, QW), 1)
    tile_row = lax.broadcasted_iota(jnp.int32, (8, QCHIP), 0)

    def unit_of(u):
        h, t = u // Z, u % Z
        return h, (t + h // (HEADS_CORE - 1)) % Z

    def score_tiles(u, par):
        h, k = unit_of(u)
        g = (z + k) % Z
        queries = jnp.concatenate([q_t[h, g, 0], q_t[h, g, 1]], axis=1)
        top = [None]

        def cached(i):
            tile = jnp.dot(
                k_heads[h, pl.ds(i * 256, 256), :], queries, preferred_element_type=jnp.float32)
            scores[par][pl.ds(i * 256, 256), :] = tile
            tile_top = jnp.max(tile.reshape(32, 8, QW), axis=0)
            top[0] = tile_top if top[0] is None else jnp.maximum(top[0], tile_top)

        def fresh():
            key_pos = jnp.where(
                row < TOK_DEV, perm[blk_of(z, y, 0)], perm[blk_of(z, y, 1)]
            ) * TOK_DEV + row % TOK_DEV
            query_blk = jnp.zeros((FRESH, QW), jnp.int32)
            for j in range(Y * CORES):
                query_blk = jnp.where(lane // TOK_DEV == j, perm[g * Y * CORES + j], query_blk)
            seen = query_blk * TOK_DEV + lane % TOK_DEV >= key_pos
            tile = jnp.dot(
                k_heads[h, pl.ds(CACHED, FRESH), :], queries, preferred_element_type=jnp.float32)
            tile = jnp.where(seen, tile, -1e30)
            scores[par][pl.ds(CACHED, FRESH), :] = tile
            all_top = jnp.maximum(top[0], jnp.max(tile.reshape(FRESH // 8, 8, QW), axis=0))
            tops[par] = jnp.broadcast_to(
                jnp.max(all_top, axis=0, keepdims=True) * LOG2_SCALE, (8, QW))

        return [lambda i=i: cached(i) for i in range(CACHED // 256)] + [fresh]

    def weight_tiles(par):
        top = tops[par][0:1]
        tops[2 + par] = tops[par]

        def weigh(at, count):
            tile = scores[par][pl.ds(at, count), :]
            probs[par][pl.ds(at, count), :] = jnp.exp2(tile * LOG2_SCALE - top).astype(jnp.bfloat16)

        spans = [(i * 256, 256) for i in range(CACHED // 256)] + [(CACHED, FRESH)]
        return [lambda s=s: weigh(*s) for s in spans]

    def value_tiles(u, par, numer):
        h, _ = unit_of(u)

        def add(at, count):
            term = jnp.dot(
                v_t[h, :, pl.ds(at, count)], probs[par][pl.ds(at, count), :],
                preferred_element_type=jnp.float32)
            numer[0] = term if numer[0] is None else numer[0] + term

        def nothing():
            pass

        steps = [nothing] * 9
        for slot, at, count in ((0, 0, 768), (3, 768, 768), (6, 1536, 640)):
            steps[slot] = lambda at=at, count=count: add(at, count)
        return steps

    def merge(u):
        h, k = unit_of(u)
        g = (z + k) % Z
        for copy in reduce_y(h, g):
            copy.wait_recv()
        own, other = part_stat[h, g, y], y_stat[h, g]
        top = jnp.maximum(own[0:1], other[0:1])
        own_factor, other_factor = jnp.exp2(own[0:1] - top), jnp.exp2(other[0:1] - top)
        total = own[1:2] * own_factor + other[1:2] * other_factor
        numer = part[h, g, y] * own_factor + y_part[h, g].astype(jnp.float32) * other_factor
        z_src[h, g] = numer.astype(jnp.bfloat16)
        z_src_stat[h, g] = jnp.where(tile_row == 0, top, total)

        @pl.when(k > 0)
        def _():
            for copy in reduce_z(h, k):
                copy.start()

    def finish(h, send=None):
        for d in range(1, Z):
            for copy in reduce_z(h, d):
                copy.wait_recv()
        stats = [z_src_stat[h, z]] + [z_stat[h, d] for d in range(1, Z)]
        numers = [z_src[h, z]] + [z_part[h, d] for d in range(1, Z)]
        top = stats[0][0:1]
        for stat in stats[1:]:
            top = jnp.maximum(top, stat[0:1])
        total = jnp.zeros((1, QCHIP), jnp.float32)
        numer = jnp.zeros((HD, QCHIP), jnp.float32)
        for stat, term in zip(stats, numers):
            factor = jnp.exp2(stat[0:1] - top)
            total = total + stat[1:2] * factor
            numer = numer + term.astype(jnp.float32) * factor
        mixed = (numer / total).T.astype(jnp.bfloat16)
        w_rows = pl.ds(pl.multiple_of(h * HD, 32), HD)
        for place, half in enumerate((1 - x, x)):
            for part_index in range(2):
                for at, count in ((0, 512), (512, 384)):
                    w_cols = pl.ds(
                        pl.multiple_of(half * COLS + part_index * CHUNK + at, 128), count)
                    term = jnp.dot(mixed, w_all[w_rows, w_cols], preferred_element_type=jnp.float32)
                    for c in range(CORES):
                        acc[half, part_index, c, :, pl.ds(at, count)] += (
                            term[c * TOK_DEV:(c + 1) * TOK_DEV])
                if send is not None:
                    send(place, half, part_index)

    def step(u, par, score, weigh, value):
        lists = []
        numer = [None]
        old_top = tops[2 + par] if value else None
        if score:
            h, k = unit_of(u)
            d = (Z - k) % Z
            gather_y(h, d).wait_recv()

            @pl.when((k > 0) & (h < HEADS_CORE - 1))
            def _():
                forward(h + 1, d)

        if value:
            lists.append(value_tiles(u - 2, par, numer))
        if weigh:
            lists.append(weight_tiles(1 - par))
        if score:
            lists.append(score_tiles(u, par))
        for group in zip(*lists):
            for work in group:
                work()
        if value:
            h, k = unit_of(u - 2)
            g = (z + k) % Z
            for j in range(Y):
                cols = slice(j * QCHIP, (j + 1) * QCHIP)
                part[h, g, j] = numer[0][:HD, cols]
                part_16[h, g, j] = numer[0][:HD, cols].astype(jnp.bfloat16)
                part_stat[h, g, j] = jnp.where(
                    tile_row == 0, old_top[:, cols], numer[0][HD:HD + 1, cols])
            for copy in reduce_y(h, g):
                copy.start()

    def beside(u):
        @pl.when((u % Z == 2) & (u < UNITS - Z))
        def _():
            prepare_keys(u // Z + 1)
            prepare_values(u // Z + 1)

        @pl.when(u >= 2 + LAG)
        def _():
            merge(u - 2 - LAG)

        @pl.when((u >= 10) & (u % Z == 2))
        def _():
            finish((u - 10) // Z)

    arrived(1)
    arrived(2)
    prepare_keys(0)
    for d in range(1, Z):
        forward(0, d)
    arrived(3)
    arrived(4)
    prepare_values(0)
    w_copy.wait()

    step(0, 0, True, False, False)
    step(1, 1, True, True, False)

    @pl.loop(1, UNITS // 2)
    def _(pair):
        for par in range(2):
            step(2 * pair + par, par, True, True, True)
            beside(2 * pair + par)

    step(UNITS, 0, False, True, True)
    merge(UNITS - 2 - LAG)
    step(UNITS + 1, 1, False, False, True)
    merge(UNITS - 1 - LAG)
    finish(HEADS_CORE - 2)
    for u in range(UNITS - LAG, UNITS):
        merge(u)

    core_out = {}

    def send_core(place, half, part_index):
        i = place * 2 + part_index
        core_out[i] = remote(
            acc.at[half, part_index, 1 - core], c_part.at[place, part_index],
            o_send.at[i], o_recv.at[i], sibling)
        core_out[i].start()

    finish(HEADS_CORE - 1, send_core)
    across = []
    for i in range(2):
        core_out[i].wait_recv()
        x_src[i] = (acc[1 - x, i, core] + c_part[0, i]).astype(jnp.bfloat16)
        copy = remote(x_src.at[i], x_part.at[i], o_send.at[4 + i], o_recv.at[4 + i], x_peer)
        copy.start()
        across.append(copy)
    for i in range(2):
        core_out[2 + i].wait_recv()
        c_part[1, i] = acc[x, i, core] + c_part[1, i]
    for i in range(2):
        across[i].wait_recv()
        out_ref[:, pl.ds(i * CHUNK, CHUNK)] = (
            c_part[1, i] + x_part[i].astype(jnp.float32)).astype(jnp.bfloat16)

    for copy in core_copies + list(core_out.values()) + across:
        copy.wait_send()

    @pl.loop(0, HEADS_CORE)
    def _(h):
        for d in range(Z):
            gather_y(h, d).wait_send()
            for copy in reduce_y(h, d):
                copy.wait_send()
            if d > 0:
                gather_z(h, d).wait_send()
                for copy in reduce_z(h, d):
                    copy.wait_send()


def fused_shards(
    queries, new_keys, new_values, key_cache, value_cache, out_weight,
    cache_len, page_table, block_perm,
):
    bf16, f32 = jnp.bfloat16, jnp.float32
    vmem, dma = pltpu.VMEM, pltpu.SemaphoreType.DMA
    hc = HEADS_CORE
    block = (HD, QCHIP)
    stat = (8, QCHIP)
    scratch = [
        vmem((CORES, TOK_DEV, GROUP), bf16),
        vmem((CORES, TOK_DEV, GROUP), bf16),
        vmem((CORES, TOK_DEV, GROUP), bf16),
        vmem((CORES, P_DEV, PAGE, GROUP), bf16),
        vmem((CORES, P_DEV, PAGE, GROUP), bf16),
        vmem((GROUP, XS * COLS), bf16),
        vmem((hc, Z, Y) + block, bf16),
        vmem((hc, KEYS, HD), bf16),
        vmem((hc, VROWS, KEYS), bf16),
        vmem((KEYS, QW), f32),
        vmem((KEYS, QW), f32),
        vmem((KEYS, QW), bf16),
        vmem((KEYS, QW), bf16),
        vmem((4, 8, QW), f32),
        vmem((hc, Z, Y) + block, f32),
        vmem((hc, Z, Y) + block, bf16),
        vmem((hc, Z, Y) + stat, f32),
        vmem((hc, Z) + block, bf16),
        vmem((hc, Z) + stat, f32),
        vmem((hc, Z) + block, bf16),
        vmem((hc, Z) + stat, f32),
        vmem((hc, Z) + block, bf16),
        vmem((hc, Z) + stat, f32),
        vmem((XS, 2, CORES, TOK_DEV, CHUNK), f32),
        vmem((2, 2, TOK_DEV, CHUNK), f32),
        vmem((2, TOK_DEV, CHUNK), bf16),
        vmem((2, TOK_DEV, CHUNK), bf16),
        dma((6,)), dma((5,)), dma((5,)),
        dma((hc, Z)), dma((hc, Z)), dma((hc, Z)), dma((hc, Z)),
        dma((hc, Z, 2)), dma((hc, Z, 2)), dma((hc, Z, 2)), dma((hc, Z, 2)),
        dma((6,)), dma((6,)),
    ]
    flops = 4 * hc * Z * QW * KEYS * HD + 2 * QCHIP * GROUP * XS * COLS
    return pl.pallas_call(
        fused_kernel,
        out_shape=jax.ShapeDtypeStruct((TOK_DEV, COLS), bf16),
        in_specs=[pl.BlockSpec(memory_space=pltpu.SMEM)] + [pl.BlockSpec(memory_space=pl.ANY)] * 6,
        out_specs=pl.BlockSpec(memory_space=pltpu.VMEM),
        scratch_shapes=scratch,
        compiler_params=pltpu.CompilerParams(
            collective_id=0, has_side_effects=True, vmem_limit_bytes=56 * 1024 * 1024),
        cost_estimate=pl.CostEstimate(
            flops=flops, bytes_accessed=14 * 1024 * 1024, transcendentals=hc * Z * QW * KEYS),
    )(block_perm, queries, new_keys, new_values, key_cache, value_cache, out_weight)


def solution(mesh):
    in_specs = (
        P("blk", "head"),
        P("blk", "head"),
        P("blk", "head"),
        P("blk", None, "head"),
        P("blk", None, "head"),
        P("head", None),
        P(),
        P(),
        P(),
    )
    out_specs = P("blk", "head")
    local = fused_shards if fits_fused(mesh) else shards
    return jax.shard_map(local, mesh=mesh, in_specs=in_specs, out_specs=out_specs, check_vma=False)
```

```python
import math

import jax
import jax.numpy as jnp
from jax import lax
from jax.experimental import pallas as pl
from jax.experimental.pallas import tpu as pltpu
from jax.sharding import PartitionSpec as P

HD = 224
PAGE = 128
P_DEV = 8
NEW = 1024
TOK_DEV = 64
MAXP = 128


def block_partial(query_rows, key_rows, value_rows, visible):
    head_count = query_rows.shape[1] // HD
    query_heads = query_rows.reshape(query_rows.shape[0], head_count, HD)
    key_heads = key_rows.reshape(key_rows.shape[0], head_count, HD)
    value_heads = value_rows.reshape(value_rows.shape[0], head_count, HD)
    scores = jnp.einsum(
        "qhd,khd->hqk", query_heads, key_heads, preferred_element_type=jnp.float32
    ) * (1.0 / math.sqrt(HD))
    scores = jnp.where(visible[None], scores, -1e30)
    row_top = jnp.max(scores, axis=2)
    weights = jnp.where(visible[None], jnp.exp(scores - row_top[:, :, None]), 0.0).astype(
        jnp.bfloat16
    )
    row_sum = jnp.sum(weights.astype(jnp.float32), axis=2)
    numerators = jnp.einsum(
        "hqk,khd->qhd", weights, value_heads, preferred_element_type=jnp.float32
    )
    return (row_top.T, row_sum.T, numerators)


def absorb(carry_state, request, partial_value):
    numer_all, top_all, sum_all = carry_state
    part_top, part_sum, part_numer = partial_value
    old_top = lax.dynamic_index_in_dim(top_all, request, 0, keepdims=False)
    old_sum = lax.dynamic_index_in_dim(sum_all, request, 0, keepdims=False)
    old_numer = lax.dynamic_index_in_dim(numer_all, request, 0, keepdims=False)
    new_top = jnp.maximum(old_top, part_top)
    old_factor = jnp.exp(old_top - new_top)
    part_factor = jnp.exp(part_top - new_top)
    merged_sum = old_factor * old_sum + part_factor * part_sum
    merged_numer = old_numer * old_factor[:, :, None] + part_numer * part_factor[:, :, None]
    return (
        lax.dynamic_update_index_in_dim(numer_all, merged_numer, request, 0),
        lax.dynamic_update_index_in_dim(top_all, new_top, request, 0),
        lax.dynamic_update_index_in_dim(sum_all, merged_sum, request, 0),
    )


def shards(
    queries,
    new_keys,
    new_values,
    key_cache,
    value_cache,
    out_weight,
    cache_len,
    page_table,
    block_perm,
):
    row_width = queries.shape[1]
    head_count = row_width // HD
    blk_count = lax.axis_size("blk")
    my_index = lax.axis_index("blk")
    req_count = cache_len.shape[0]
    blocks_per_req = NEW // TOK_DEV
    gathered = lax.all_gather(queries, "blk", axis=0, tiled=True)
    block_ids = jnp.arange(blk_count, dtype=jnp.int32)
    inverse = jnp.zeros((blk_count,), jnp.int32).at[block_perm].set(block_ids)
    query_all = gathered.reshape(blk_count, TOK_DEV, row_width)[inverse].reshape(
        req_count, NEW, row_width
    )
    global_ids = my_index * P_DEV + jnp.arange(P_DEV, dtype=jnp.int32)
    table_ids = jnp.arange(page_table.shape[0], dtype=jnp.int32)
    match_rows = page_table[None, :] == global_ids[:, None]
    logical = jnp.sum(jnp.where(match_rows, table_ids[None, :], 0), axis=1)
    page_req = logical // MAXP
    page_pos = logical % MAXP
    page_fill = jnp.clip(cache_len[page_req] - page_pos * PAGE, 0, PAGE)
    slot_ids = jnp.arange(PAGE, dtype=jnp.int32)
    start_state = (
        jnp.zeros((req_count, NEW, head_count, HD), jnp.float32),
        jnp.full((req_count, NEW, head_count), -1e30, jnp.float32),
        jnp.zeros((req_count, NEW, head_count), jnp.float32),
    )

    def page_work(slot_index, carry_state):
        request = page_req[slot_index]
        query_rows = lax.dynamic_index_in_dim(query_all, request, 0, keepdims=False)
        key_rows = lax.dynamic_index_in_dim(key_cache, slot_index, 0, keepdims=False)
        value_rows = lax.dynamic_index_in_dim(value_cache, slot_index, 0, keepdims=False)
        visible = jnp.broadcast_to((slot_ids < page_fill[slot_index])[None, :], (NEW, PAGE))
        return absorb(
            carry_state, request, block_partial(query_rows, key_rows, value_rows, visible)
        )

    def page_step(slot_index, carry_state):
        return page_work(slot_index, carry_state)

    carry_state = lax.fori_loop(0, P_DEV, page_step, start_state)
    my_block = block_perm[my_index]
    my_request = my_block // blocks_per_req
    my_offset = my_block % blocks_per_req * TOK_DEV
    new_pos = jnp.arange(NEW, dtype=jnp.int32)[:, None]
    key_pos = my_offset + jnp.arange(TOK_DEV, dtype=jnp.int32)[None, :]
    own_rows = lax.dynamic_index_in_dim(query_all, my_request, 0, keepdims=False)
    carry_state = absorb(
        carry_state, my_request, block_partial(own_rows, new_keys, new_values, new_pos >= key_pos)
    )
    numer_all, top_all, sum_all = carry_state
    send_numer = numer_all.reshape(blk_count, TOK_DEV, row_width)[block_perm]
    send_top = top_all.reshape(blk_count, TOK_DEV, head_count)[block_perm]
    send_sum = sum_all.reshape(blk_count, TOK_DEV, head_count)[block_perm]
    recv_numer, recv_top, recv_sum = (
        lax.all_to_all(send_numer, "blk", split_axis=0, concat_axis=0, tiled=True),
        lax.all_to_all(send_top, "blk", split_axis=0, concat_axis=0, tiled=True),
        lax.all_to_all(send_sum, "blk", split_axis=0, concat_axis=0, tiled=True),
    )
    best_top = jnp.max(recv_top, axis=0)
    factor = jnp.exp(recv_top - best_top[None])
    total_sum = jnp.sum(recv_sum * factor, axis=0)
    total_numer = jnp.sum(
        recv_numer.reshape(blk_count, TOK_DEV, head_count, HD) * factor[..., None], axis=0
    )
    mixed = (total_numer / total_sum[:, :, None]).reshape(TOK_DEV, row_width).astype(jnp.bfloat16)
    head_term = jnp.dot(mixed, out_weight, preferred_element_type=jnp.float32)
    return lax.psum_scatter(head_term, "head", scatter_dimension=1, tiled=True).astype(jnp.bfloat16)


MESH = pl.DeviceIdType.MESH
Z, Y, CORES, XS = 4, 2, 2, 2
HEADS_CORE = 4
GROUP = HEADS_CORE * HD
CACHED = CORES * P_DEV * PAGE
FRESH = CORES * TOK_DEV
KEYS = CACHED + FRESH
QCHIP = CORES * TOK_DEV
QW = Y * QCHIP
VROWS = HD + 16
COLS = 1792
CHUNK = COLS // 2
WINDOW = 384
UNITS = HEADS_CORE * Z
LAG = 2
LOG2_SCALE = math.log2(math.e) / math.sqrt(HD)


def fits_fused(mesh):
    return dict(mesh.shape) == {"blk": Z * Y * CORES, "head": XS}


def fused_kernel(
    perm, q_hbm, nk_hbm, nv_hbm, kc_hbm, vc_hbm, w_hbm, out_ref,
    q_stage, nk_stage, nv_stage, k_stage, v_stage, w_all,
    q_t, k_heads, v_t, scores_a, scores_b, probs_a, probs_b, tops,
    part, part_16, part_stat, y_part, y_stat,
    z_src, z_src_stat, z_part, z_stat,
    acc, c_part, x_src, x_part,
    local_sem, core_send, core_recv, gz_send, gz_recv, gy_send, gy_recv,
    ry_send, ry_recv, rz_send, rz_recv, o_send, o_recv,
):
    me = lax.axis_index("blk")
    x = lax.axis_index("head")
    core = me % CORES
    y = (me // CORES) % Y
    z = me // (CORES * Y)
    scores, probs = (scores_a, scores_b), (probs_a, probs_b)

    def blk_of(zz, yy, cc):
        return (zz * Y + yy) * CORES + cc

    sibling = (blk_of(z, y, 1 - core), x)
    y_peer = (blk_of(z, 1 - y, core), x)
    x_peer = (me, 1 - x)

    def z_to(d):
        return (blk_of((z + d) % Z, y, core), x)

    barrier = pltpu.get_barrier_semaphore()
    for peer in [sibling, y_peer, x_peer] + [z_to(d) for d in range(1, Z)]:
        pl.semaphore_signal(barrier, inc=1, device_id=peer, device_id_type=MESH)
    pl.semaphore_wait(barrier, Z + 2)

    def remote(src, dst, send_sem, recv_sem, peer):
        return pltpu.make_async_remote_copy(
            src_ref=src, dst_ref=dst, send_sem=send_sem, recv_sem=recv_sem,
            device_id=peer, device_id_type=MESH)

    mine = pl.ds(pl.multiple_of(core * GROUP, 128), GROUP)
    theirs = pl.ds(pl.multiple_of((1 - core) * GROUP, 128), GROUP)
    staged = [
        (q_hbm, q_stage), (kc_hbm, k_stage), (nk_hbm, nk_stage),
        (vc_hbm, v_stage), (nv_hbm, nv_stage),
    ]
    local_copies, core_copies = [], []
    for i, (src, dst) in enumerate(staged):
        lead = (slice(None),) * (len(src.shape) - 1)
        copy = remote(
            src.at[lead + (theirs,)], dst.at[core], core_send.at[i], core_recv.at[i], sibling)
        copy.start()
        core_copies.append(copy)
        copy = pltpu.make_async_copy(src.at[lead + (mine,)], dst.at[core], local_sem.at[i])
        copy.start()
        local_copies.append(copy)
    w_copy = pltpu.make_async_copy(
        w_hbm.at[pl.ds(pl.multiple_of(core * GROUP, 128), GROUP), :], w_all, local_sem.at[5])
    w_copy.start()

    def arrived(i):
        local_copies[i].wait()
        core_copies[i].wait_recv()

    def gather_z(h, d):
        block = q_t.at[h, z, y]
        return remote(block, block, gz_send.at[h, d], gz_recv.at[h, d], z_to(d))

    def gather_y(h, d):
        block = q_t.at[h, (z + Z - d) % Z, y]
        return remote(block, block, gy_send.at[h, d], gy_recv.at[h, d], y_peer)

    def forward(h, d):
        gather_z(h, d).wait_recv()
        gather_y(h, d).start()

    def reduce_y(h, g):
        return (
            remote(part_16.at[h, g, 1 - y], y_part.at[h, g],
                   ry_send.at[h, g, 0], ry_recv.at[h, g, 0], y_peer),
            remote(part_stat.at[h, g, 1 - y], y_stat.at[h, g],
                   ry_send.at[h, g, 1], ry_recv.at[h, g, 1], y_peer),
        )

    def reduce_z(h, d):
        to = (z + d) % Z
        return (
            remote(z_src.at[h, to], z_part.at[h, d],
                   rz_send.at[h, d, 0], rz_recv.at[h, d, 0], z_to(d)),
            remote(z_src_stat.at[h, to], z_stat.at[h, d],
                   rz_send.at[h, d, 1], rz_recv.at[h, d, 1], z_to(d)),
        )

    arrived(0)
    q_rows = jnp.concatenate([q_stage[0], q_stage[1]], axis=0).astype(jnp.float32)
    q_cols = q_rows.T.astype(jnp.bfloat16)
    for h in range(HEADS_CORE):
        q_t[h, z, y] = q_cols[h * HD:(h + 1) * HD]

    def send_queries(h):
        for d in range(1, Z):
            gather_z(h, d).start()
        gather_y(h, 0).start()

    send_queries(0)

    v_t[:, pl.ds(HD, VROWS - HD), :] = jnp.ones((HEADS_CORE, VROWS - HD, KEYS), jnp.bfloat16)
    acc[...] = jnp.zeros(acc.shape, jnp.float32)

    def head_window(h):
        start = jnp.minimum(h * HD // 128 * 128, GROUP - WINDOW)
        return pl.ds(pl.multiple_of(start, 128), WINDOW), h * HD - start

    def prepare_keys(h):
        window, offset = head_window(h)
        pick = jnp.where(
            lax.broadcasted_iota(jnp.int32, (WINDOW, HD), 0)
            == lax.broadcasted_iota(jnp.int32, (WINDOW, HD), 1) + offset, 1.0, 0.0
        ).astype(jnp.bfloat16)

        def place(rows, at, count):
            k_heads[h, pl.ds(at, count), :] = jnp.dot(
                rows, pick, preferred_element_type=jnp.float32).astype(jnp.bfloat16)

        for c in range(CORES):
            for page in range(0, P_DEV, 2):
                rows = k_stage[c, pl.ds(page, 2), :, window].reshape(2 * PAGE, WINDOW)
                place(rows, (c * P_DEV + page) * PAGE, 2 * PAGE)
            place(nk_stage[c, :, window], CACHED + c * TOK_DEV, TOK_DEV)

    def prepare_values(h):
        window, offset = head_window(h)
        pick = jnp.where(
            lax.broadcasted_iota(jnp.int32, (HD, WINDOW), 1)
            == lax.broadcasted_iota(jnp.int32, (HD, WINDOW), 0) + offset, 1.0, 0.0
        ).astype(jnp.bfloat16)

        def place(rows, at, count):
            v_t[h, pl.ds(0, HD), pl.ds(at, count)] = lax.dot_general(
                pick, rows, (((1,), (1,)), ((), ())), preferred_element_type=jnp.float32
            ).astype(jnp.bfloat16)

        for c in range(CORES):
            for page in range(0, P_DEV, 2):
                rows = v_stage[c, pl.ds(page, 2), :, window].reshape(2 * PAGE, WINDOW)
                place(rows, (c * P_DEV + page) * PAGE, 2 * PAGE)
        place(jnp.concatenate([nv_stage[c, :, window] for c in range(CORES)], axis=0), CACHED, FRESH)

    row = lax.broadcasted_iota(jnp.int32, (FRESH, QW), 0)
    lane = lax.broadcasted_iota(jnp.int32, (FRESH, QW), 1)
    tile_row = lax.broadcasted_iota(jnp.int32, (2, QCHIP), 0)

    def unit_of(u):
        h, t = u // Z, u % Z
        return h, (t + h // (HEADS_CORE - 1)) % Z

    def score_tiles(u, par):
        h, k = unit_of(u)
        g = (z + k) % Z
        queries = jnp.concatenate([q_t[h, g, 0], q_t[h, g, 1]], axis=1)
        top = [None]

        def cached(i):
            tile = jnp.dot(
                k_heads[h, pl.ds(i * 256, 256), :], queries, preferred_element_type=jnp.float32)
            scores[par][pl.ds(i * 256, 256), :] = tile
            tile_top = jnp.max(tile.reshape(32, 8, QW), axis=0)
            top[0] = tile_top if top[0] is None else jnp.maximum(top[0], tile_top)

        def fresh():
            key_pos = jnp.where(
                row < TOK_DEV, perm[blk_of(z, y, 0)], perm[blk_of(z, y, 1)]
            ) * TOK_DEV + row % TOK_DEV
            query_blk = jnp.zeros((FRESH, QW), jnp.int32)
            for j in range(Y * CORES):
                query_blk = jnp.where(lane // TOK_DEV == j, perm[g * Y * CORES + j], query_blk)
            seen = query_blk * TOK_DEV + lane % TOK_DEV >= key_pos
            tile = jnp.dot(
                k_heads[h, pl.ds(CACHED, FRESH), :], queries, preferred_element_type=jnp.float32)
            tile = jnp.where(seen, tile, -1e30)
            scores[par][pl.ds(CACHED, FRESH), :] = tile
            all_top = jnp.maximum(top[0], jnp.max(tile.reshape(FRESH // 8, 8, QW), axis=0))
            tops[par] = jnp.broadcast_to(
                jnp.max(all_top, axis=0, keepdims=True) * LOG2_SCALE, (8, QW))

        return [lambda i=i: cached(i) for i in range(CACHED // 256)] + [fresh]

    def weight_tiles(par):
        top = tops[par][0:1]
        tops[2 + par] = tops[par]

        def weigh(at, count):
            tile = scores[par][pl.ds(at, count), :]
            probs[par][pl.ds(at, count), :] = jnp.exp2(tile * LOG2_SCALE - top).astype(jnp.bfloat16)

        spans = [(i * 256, 256) for i in range(CACHED // 256)] + [(CACHED, FRESH)]
        return [lambda s=s: weigh(*s) for s in spans]

    def value_tiles(u, par, numer):
        h, _ = unit_of(u)

        def add(at, count):
            term = jnp.dot(
                v_t[h, :, pl.ds(at, count)], probs[par][pl.ds(at, count), :],
                preferred_element_type=jnp.float32)
            numer[0] = term if numer[0] is None else numer[0] + term

        def nothing():
            pass

        steps = [nothing] * 9
        for slot, at, count in ((0, 0, 768), (3, 768, 768), (6, 1536, 640)):
            steps[slot] = lambda at=at, count=count: add(at, count)
        return steps

    def merge(u):
        h, k = unit_of(u)
        g = (z + k) % Z
        for copy in reduce_y(h, g):
            copy.wait_recv()
        own, other = part_stat[h, g, y], y_stat[h, g]
        top = jnp.maximum(own[0:1], other[0:1])
        own_factor, other_factor = jnp.exp2(own[0:1] - top), jnp.exp2(other[0:1] - top)
        total = own[1:2] * own_factor + other[1:2] * other_factor
        numer = part[h, g, y] * own_factor + y_part[h, g].astype(jnp.float32) * other_factor
        z_src[h, g] = numer.astype(jnp.bfloat16)
        z_src_stat[h, g] = jnp.where(tile_row == 0, top, total)

        @pl.when(k > 0)
        def _():
            for copy in reduce_z(h, k):
                copy.start()

    def finish(h, send=None):
        for d in range(1, Z):
            for copy in reduce_z(h, d):
                copy.wait_recv()
        stats = [z_src_stat[h, z]] + [z_stat[h, d] for d in range(1, Z)]
        numers = [z_src[h, z]] + [z_part[h, d] for d in range(1, Z)]
        top = stats[0][0:1]
        for stat in stats[1:]:
            top = jnp.maximum(top, stat[0:1])
        total = jnp.zeros((1, QCHIP), jnp.float32)
        numer = jnp.zeros((HD, QCHIP), jnp.float32)
        for stat, term in zip(stats, numers):
            factor = jnp.exp2(stat[0:1] - top)
            total = total + stat[1:2] * factor
            numer = numer + term.astype(jnp.float32) * factor
        mixed = (numer / total).T.astype(jnp.bfloat16)
        w_rows = pl.ds(pl.multiple_of(h * HD, 32), HD)
        for place, half in enumerate((1 - x, x)):
            for part_index in range(2):
                for at, count in ((0, 512), (512, 384)):
                    w_cols = pl.ds(
                        pl.multiple_of(half * COLS + part_index * CHUNK + at, 128), count)
                    term = jnp.dot(mixed, w_all[w_rows, w_cols], preferred_element_type=jnp.float32)
                    for c in range(CORES):
                        acc[half, part_index, c, :, pl.ds(at, count)] += (
                            term[c * TOK_DEV:(c + 1) * TOK_DEV])
                if send is not None:
                    send(place, half, part_index)

    def step(u, par, score, weigh, value):
        lists = []
        numer = [None]
        old_top = tops[2 + par][0:1] if value else None
        if score:
            h, k = unit_of(u)
            d = (Z - k) % Z
            gather_y(h, d).wait_recv()

            @pl.when((k > 0) & (h < HEADS_CORE - 1))
            def _():
                forward(h + 1, d)

            @pl.when((k == 1) & (h < HEADS_CORE - 2))
            def _():
                send_queries(h + 2)

        if value:
            lists.append(value_tiles(u - 2, par, numer))
        if weigh:
            lists.append(weight_tiles(1 - par))
        if score:
            lists.append(score_tiles(u, par))
        for group in zip(*lists):
            for work in group:
                work()
        if value:
            h, k = unit_of(u - 2)
            g = (z + k) % Z
            for j in range(Y):
                cols = slice(j * QCHIP, (j + 1) * QCHIP)
                part[h, g, j] = numer[0][:HD, cols]
                part_16[h, g, j] = numer[0][:HD, cols].astype(jnp.bfloat16)
                part_stat[h, g, j] = jnp.where(
                    tile_row == 0, old_top[:, cols], numer[0][HD:HD + 1, cols])
            for copy in reduce_y(h, g):
                copy.start()

    def beside(u):
        @pl.when((u % Z == 2) & (u < UNITS - Z))
        def _():
            prepare_keys(u // Z + 1)
            prepare_values(u // Z + 1)

        @pl.when(u >= 2 + LAG)
        def _():
            merge(u - 2 - LAG)

        @pl.when((u >= 10) & (u % Z == 2))
        def _():
            finish((u - 10) // Z)

    arrived(1)
    arrived(2)
    prepare_keys(0)
    for d in range(1, Z):
        forward(0, d)
    send_queries(1)
    arrived(3)
    arrived(4)
    prepare_values(0)
    w_copy.wait()

    step(0, 0, True, False, False)
    step(1, 1, True, True, False)

    @pl.loop(1, UNITS // 2)
    def _(pair):
        for par in range(2):
            step(2 * pair + par, par, True, True, True)
            beside(2 * pair + par)

    step(UNITS, 0, False, True, True)
    merge(UNITS - 2 - LAG)
    step(UNITS + 1, 1, False, False, True)
    merge(UNITS - 1 - LAG)
    finish(HEADS_CORE - 2)
    for u in range(UNITS - LAG, UNITS):
        merge(u)

    core_out = {}

    def send_core(place, half, part_index):
        i = place * 2 + part_index
        core_out[i] = remote(
            acc.at[half, part_index, 1 - core], c_part.at[place, part_index],
            o_send.at[i], o_recv.at[i], sibling)
        core_out[i].start()

    finish(HEADS_CORE - 1, send_core)
    across = []
    for i in range(2):
        core_out[i].wait_recv()
        x_src[i] = (acc[1 - x, i, core] + c_part[0, i]).astype(jnp.bfloat16)
        copy = remote(x_src.at[i], x_part.at[i], o_send.at[4 + i], o_recv.at[4 + i], x_peer)
        copy.start()
        across.append(copy)
    for i in range(2):
        core_out[2 + i].wait_recv()
        c_part[1, i] = acc[x, i, core] + c_part[1, i]
    for i in range(2):
        across[i].wait_recv()
        out_ref[:, pl.ds(i * CHUNK, CHUNK)] = (
            c_part[1, i] + x_part[i].astype(jnp.float32)).astype(jnp.bfloat16)

    for copy in core_copies + list(core_out.values()) + across:
        copy.wait_send()

    @pl.loop(0, HEADS_CORE)
    def _(h):
        for d in range(Z):
            gather_y(h, d).wait_send()
            for copy in reduce_y(h, d):
                copy.wait_send()
            if d > 0:
                gather_z(h, d).wait_send()
                for copy in reduce_z(h, d):
                    copy.wait_send()


def fused_shards(
    queries, new_keys, new_values, key_cache, value_cache, out_weight,
    cache_len, page_table, block_perm,
):
    bf16, f32 = jnp.bfloat16, jnp.float32
    vmem, dma = pltpu.VMEM, pltpu.SemaphoreType.DMA
    hc = HEADS_CORE
    block = (HD, QCHIP)
    stat = (2, QCHIP)
    scratch = [
        vmem((CORES, TOK_DEV, GROUP), bf16),
        vmem((CORES, TOK_DEV, GROUP), bf16),
        vmem((CORES, TOK_DEV, GROUP), bf16),
        vmem((CORES, P_DEV, PAGE, GROUP), bf16),
        vmem((CORES, P_DEV, PAGE, GROUP), bf16),
        vmem((GROUP, XS * COLS), bf16),
        vmem((hc, Z, Y) + block, bf16),
        vmem((hc, KEYS, HD), bf16),
        vmem((hc, VROWS, KEYS), bf16),
        vmem((KEYS, QW), f32),
        vmem((KEYS, QW), f32),
        vmem((KEYS, QW), bf16),
        vmem((KEYS, QW), bf16),
        vmem((4, 8, QW), f32),
        vmem((hc, Z, Y) + block, f32),
        vmem((hc, Z, Y) + block, bf16),
        vmem((hc, Z, Y) + stat, f32),
        vmem((hc, Z) + block, bf16),
        vmem((hc, Z) + stat, f32),
        vmem((hc, Z) + block, bf16),
        vmem((hc, Z) + stat, f32),
        vmem((hc, Z) + block, bf16),
        vmem((hc, Z) + stat, f32),
        vmem((XS, 2, CORES, TOK_DEV, CHUNK), f32),
        vmem((2, 2, TOK_DEV, CHUNK), f32),
        vmem((2, TOK_DEV, CHUNK), bf16),
        vmem((2, TOK_DEV, CHUNK), bf16),
        dma((6,)), dma((5,)), dma((5,)),
        dma((hc, Z)), dma((hc, Z)), dma((hc, Z)), dma((hc, Z)),
        dma((hc, Z, 2)), dma((hc, Z, 2)), dma((hc, Z, 2)), dma((hc, Z, 2)),
        dma((6,)), dma((6,)),
    ]
    flops = 4 * hc * Z * QW * KEYS * HD + 2 * QCHIP * GROUP * XS * COLS
    return pl.pallas_call(
        fused_kernel,
        out_shape=jax.ShapeDtypeStruct((TOK_DEV, COLS), bf16),
        in_specs=[pl.BlockSpec(memory_space=pltpu.SMEM)] + [pl.BlockSpec(memory_space=pl.ANY)] * 6,
        out_specs=pl.BlockSpec(memory_space=pltpu.VMEM),
        scratch_shapes=scratch,
        compiler_params=pltpu.CompilerParams(
            collective_id=0, has_side_effects=True, vmem_limit_bytes=56 * 1024 * 1024),
        cost_estimate=pl.CostEstimate(
            flops=flops, bytes_accessed=14 * 1024 * 1024, transcendentals=hc * Z * QW * KEYS),
    )(block_perm, queries, new_keys, new_values, key_cache, value_cache, out_weight)


def solution(mesh):
    in_specs = (
        P("blk", "head"),
        P("blk", "head"),
        P("blk", "head"),
        P("blk", None, "head"),
        P("blk", None, "head"),
        P("head", None),
        P(),
        P(),
        P(),
    )
    out_specs = P("blk", "head")
    local = fused_shards if fits_fused(mesh) else shards
    return jax.shard_map(local, mesh=mesh, in_specs=in_specs, out_specs=out_specs, check_vma=False)
```

```python
import math

import jax
import jax.numpy as jnp
from jax import lax
from jax.experimental import pallas as pl
from jax.experimental.pallas import tpu as pltpu
from jax.sharding import PartitionSpec as P

HD = 224
PAGE = 128
P_DEV = 8
NEW = 1024
TOK_DEV = 64
MAXP = 128


def block_partial(query_rows, key_rows, value_rows, visible):
    head_count = query_rows.shape[1] // HD
    query_heads = query_rows.reshape(query_rows.shape[0], head_count, HD)
    key_heads = key_rows.reshape(key_rows.shape[0], head_count, HD)
    value_heads = value_rows.reshape(value_rows.shape[0], head_count, HD)
    scores = jnp.einsum(
        "qhd,khd->hqk", query_heads, key_heads, preferred_element_type=jnp.float32
    ) * (1.0 / math.sqrt(HD))
    scores = jnp.where(visible[None], scores, -1e30)
    row_top = jnp.max(scores, axis=2)
    weights = jnp.where(visible[None], jnp.exp(scores - row_top[:, :, None]), 0.0).astype(
        jnp.bfloat16
    )
    row_sum = jnp.sum(weights.astype(jnp.float32), axis=2)
    numerators = jnp.einsum(
        "hqk,khd->qhd", weights, value_heads, preferred_element_type=jnp.float32
    )
    return (row_top.T, row_sum.T, numerators)


def absorb(carry_state, request, partial_value):
    numer_all, top_all, sum_all = carry_state
    part_top, part_sum, part_numer = partial_value
    old_top = lax.dynamic_index_in_dim(top_all, request, 0, keepdims=False)
    old_sum = lax.dynamic_index_in_dim(sum_all, request, 0, keepdims=False)
    old_numer = lax.dynamic_index_in_dim(numer_all, request, 0, keepdims=False)
    new_top = jnp.maximum(old_top, part_top)
    old_factor = jnp.exp(old_top - new_top)
    part_factor = jnp.exp(part_top - new_top)
    merged_sum = old_factor * old_sum + part_factor * part_sum
    merged_numer = old_numer * old_factor[:, :, None] + part_numer * part_factor[:, :, None]
    return (
        lax.dynamic_update_index_in_dim(numer_all, merged_numer, request, 0),
        lax.dynamic_update_index_in_dim(top_all, new_top, request, 0),
        lax.dynamic_update_index_in_dim(sum_all, merged_sum, request, 0),
    )


def shards(
    queries,
    new_keys,
    new_values,
    key_cache,
    value_cache,
    out_weight,
    cache_len,
    page_table,
    block_perm,
):
    row_width = queries.shape[1]
    head_count = row_width // HD
    blk_count = lax.axis_size("blk")
    my_index = lax.axis_index("blk")
    req_count = cache_len.shape[0]
    blocks_per_req = NEW // TOK_DEV
    gathered = lax.all_gather(queries, "blk", axis=0, tiled=True)
    block_ids = jnp.arange(blk_count, dtype=jnp.int32)
    inverse = jnp.zeros((blk_count,), jnp.int32).at[block_perm].set(block_ids)
    query_all = gathered.reshape(blk_count, TOK_DEV, row_width)[inverse].reshape(
        req_count, NEW, row_width
    )
    global_ids = my_index * P_DEV + jnp.arange(P_DEV, dtype=jnp.int32)
    table_ids = jnp.arange(page_table.shape[0], dtype=jnp.int32)
    match_rows = page_table[None, :] == global_ids[:, None]
    logical = jnp.sum(jnp.where(match_rows, table_ids[None, :], 0), axis=1)
    page_req = logical // MAXP
    page_pos = logical % MAXP
    page_fill = jnp.clip(cache_len[page_req] - page_pos * PAGE, 0, PAGE)
    slot_ids = jnp.arange(PAGE, dtype=jnp.int32)
    start_state = (
        jnp.zeros((req_count, NEW, head_count, HD), jnp.float32),
        jnp.full((req_count, NEW, head_count), -1e30, jnp.float32),
        jnp.zeros((req_count, NEW, head_count), jnp.float32),
    )

    def page_work(slot_index, carry_state):
        request = page_req[slot_index]
        query_rows = lax.dynamic_index_in_dim(query_all, request, 0, keepdims=False)
        key_rows = lax.dynamic_index_in_dim(key_cache, slot_index, 0, keepdims=False)
        value_rows = lax.dynamic_index_in_dim(value_cache, slot_index, 0, keepdims=False)
        visible = jnp.broadcast_to((slot_ids < page_fill[slot_index])[None, :], (NEW, PAGE))
        return absorb(
            carry_state, request, block_partial(query_rows, key_rows, value_rows, visible)
        )

    def page_step(slot_index, carry_state):
        return page_work(slot_index, carry_state)

    carry_state = lax.fori_loop(0, P_DEV, page_step, start_state)
    my_block = block_perm[my_index]
    my_request = my_block // blocks_per_req
    my_offset = my_block % blocks_per_req * TOK_DEV
    new_pos = jnp.arange(NEW, dtype=jnp.int32)[:, None]
    key_pos = my_offset + jnp.arange(TOK_DEV, dtype=jnp.int32)[None, :]
    own_rows = lax.dynamic_index_in_dim(query_all, my_request, 0, keepdims=False)
    carry_state = absorb(
        carry_state, my_request, block_partial(own_rows, new_keys, new_values, new_pos >= key_pos)
    )
    numer_all, top_all, sum_all = carry_state
    send_numer = numer_all.reshape(blk_count, TOK_DEV, row_width)[block_perm]
    send_top = top_all.reshape(blk_count, TOK_DEV, head_count)[block_perm]
    send_sum = sum_all.reshape(blk_count, TOK_DEV, head_count)[block_perm]
    recv_numer, recv_top, recv_sum = (
        lax.all_to_all(send_numer, "blk", split_axis=0, concat_axis=0, tiled=True),
        lax.all_to_all(send_top, "blk", split_axis=0, concat_axis=0, tiled=True),
        lax.all_to_all(send_sum, "blk", split_axis=0, concat_axis=0, tiled=True),
    )
    best_top = jnp.max(recv_top, axis=0)
    factor = jnp.exp(recv_top - best_top[None])
    total_sum = jnp.sum(recv_sum * factor, axis=0)
    total_numer = jnp.sum(
        recv_numer.reshape(blk_count, TOK_DEV, head_count, HD) * factor[..., None], axis=0
    )
    mixed = (total_numer / total_sum[:, :, None]).reshape(TOK_DEV, row_width).astype(jnp.bfloat16)
    head_term = jnp.dot(mixed, out_weight, preferred_element_type=jnp.float32)
    return lax.psum_scatter(head_term, "head", scatter_dimension=1, tiled=True).astype(jnp.bfloat16)


MESH = pl.DeviceIdType.MESH
Z, Y, CORES, XS = 4, 2, 2, 2
HEADS_CORE = 4
GROUP = HEADS_CORE * HD
CACHED = CORES * P_DEV * PAGE
FRESH = CORES * TOK_DEV
KEYS = CACHED + FRESH
QCHIP = CORES * TOK_DEV
QW = Y * QCHIP
VROWS = HD + 16
COLS = 1792
CHUNK = COLS // 2
WINDOW = 384
UNITS = HEADS_CORE * Z
LAG = 2
LOG2_SCALE = math.log2(math.e) / math.sqrt(HD)


def fits_fused(mesh):
    return dict(mesh.shape) == {"blk": Z * Y * CORES, "head": XS}


def fused_kernel(
    perm, q_hbm, nk_hbm, nv_hbm, kc_hbm, vc_hbm, w_hbm, out_ref,
    q_stage, nk_stage, nv_stage, k_stage, v_stage, w_all,
    q_t, k_heads, v_t, scores_a, scores_b, probs_a, probs_b, tops,
    part, part_16, part_stat, y_part, y_stat,
    z_src, z_src_stat, z_part, z_stat,
    acc, c_part, x_src, x_part,
    local_sem, core_send, core_recv, gz_send, gz_recv, gy_send, gy_recv,
    ry_send, ry_recv, rz_send, rz_recv, o_send, o_recv,
):
    me = lax.axis_index("blk")
    x = lax.axis_index("head")
    core = me % CORES
    y = (me // CORES) % Y
    z = me // (CORES * Y)
    scores, probs = (scores_a, scores_b), (probs_a, probs_b)

    def blk_of(zz, yy, cc):
        return (zz * Y + yy) * CORES + cc

    sibling = (blk_of(z, y, 1 - core), x)
    y_peer = (blk_of(z, 1 - y, core), x)
    x_peer = (me, 1 - x)

    def z_to(d):
        return (blk_of((z + d) % Z, y, core), x)

    barrier = pltpu.get_barrier_semaphore()
    for peer in [sibling, y_peer, x_peer] + [z_to(d) for d in range(1, Z)]:
        pl.semaphore_signal(barrier, inc=1, device_id=peer, device_id_type=MESH)
    pl.semaphore_wait(barrier, Z + 2)

    def remote(src, dst, send_sem, recv_sem, peer):
        return pltpu.make_async_remote_copy(
            src_ref=src, dst_ref=dst, send_sem=send_sem, recv_sem=recv_sem,
            device_id=peer, device_id_type=MESH)

    mine = pl.ds(pl.multiple_of(core * GROUP, 128), GROUP)
    theirs = pl.ds(pl.multiple_of((1 - core) * GROUP, 128), GROUP)
    staged = [
        (q_hbm, q_stage), (kc_hbm, k_stage), (nk_hbm, nk_stage),
        (vc_hbm, v_stage), (nv_hbm, nv_stage),
    ]
    local_copies, core_copies = [], []
    for i, (src, dst) in enumerate(staged):
        lead = (slice(None),) * (len(src.shape) - 1)
        copy = remote(
            src.at[lead + (theirs,)], dst.at[core], core_send.at[i], core_recv.at[i], sibling)
        copy.start()
        core_copies.append(copy)
        copy = pltpu.make_async_copy(src.at[lead + (mine,)], dst.at[core], local_sem.at[i])
        copy.start()
        local_copies.append(copy)
    w_copy = pltpu.make_async_copy(
        w_hbm.at[pl.ds(pl.multiple_of(core * GROUP, 128), GROUP), :], w_all, local_sem.at[5])
    w_copy.start()

    def arrived(i):
        local_copies[i].wait()
        core_copies[i].wait_recv()

    def gather_z(h, d):
        block = q_t.at[h, z, y]
        return remote(block, block, gz_send.at[h, d], gz_recv.at[h, d], z_to(d))

    def gather_y(h, d):
        block = q_t.at[h, (z + Z - d) % Z, y]
        return remote(block, block, gy_send.at[h, d], gy_recv.at[h, d], y_peer)

    def forward(h, d):
        gather_z(h, d).wait_recv()
        gather_y(h, d).start()

    def reduce_y(h, g):
        return (
            remote(part_16.at[h, g, 1 - y], y_part.at[h, g],
                   ry_send.at[h, g, 0], ry_recv.at[h, g, 0], y_peer),
            remote(part_stat.at[h, g, 1 - y], y_stat.at[h, g],
                   ry_send.at[h, g, 1], ry_recv.at[h, g, 1], y_peer),
        )

    def reduce_z(h, d):
        to = (z + d) % Z
        return (
            remote(z_src.at[h, to], z_part.at[h, d],
                   rz_send.at[h, d, 0], rz_recv.at[h, d, 0], z_to(d)),
            remote(z_src_stat.at[h, to], z_stat.at[h, d],
                   rz_send.at[h, d, 1], rz_recv.at[h, d, 1], z_to(d)),
        )

    arrived(0)
    q_rows = jnp.concatenate([q_stage[0], q_stage[1]], axis=0).astype(jnp.float32)
    q_cols = q_rows.T.astype(jnp.bfloat16)
    for h in range(HEADS_CORE):
        q_t[h, z, y] = q_cols[h * HD:(h + 1) * HD]

    def send_queries(h):
        for d in range(1, Z):
            gather_z(h, d).start()
        gather_y(h, 0).start()

    send_queries(0)

    v_t[:, pl.ds(HD, VROWS - HD), :] = jnp.ones((HEADS_CORE, VROWS - HD, KEYS), jnp.bfloat16)
    acc[...] = jnp.zeros(acc.shape, jnp.float32)

    def head_window(h):
        start = jnp.minimum(h * HD // 128 * 128, GROUP - WINDOW)
        return pl.ds(pl.multiple_of(start, 128), WINDOW), h * HD - start

    def prepare_keys(h):
        window, offset = head_window(h)
        pick = jnp.where(
            lax.broadcasted_iota(jnp.int32, (WINDOW, HD), 0)
            == lax.broadcasted_iota(jnp.int32, (WINDOW, HD), 1) + offset, 1.0, 0.0
        ).astype(jnp.bfloat16)

        def place(rows, at, count):
            k_heads[h, pl.ds(at, count), :] = jnp.dot(
                rows, pick, preferred_element_type=jnp.float32).astype(jnp.bfloat16)

        for c in range(CORES):
            for page in range(0, P_DEV, 2):
                rows = k_stage[c, pl.ds(page, 2), :, window].reshape(2 * PAGE, WINDOW)
                place(rows, (c * P_DEV + page) * PAGE, 2 * PAGE)
            place(nk_stage[c, :, window], CACHED + c * TOK_DEV, TOK_DEV)

    def prepare_values(h):
        window, offset = head_window(h)
        pick = jnp.where(
            lax.broadcasted_iota(jnp.int32, (HD, WINDOW), 1)
            == lax.broadcasted_iota(jnp.int32, (HD, WINDOW), 0) + offset, 1.0, 0.0
        ).astype(jnp.bfloat16)

        def place(rows, at, count):
            v_t[h, pl.ds(0, HD), pl.ds(at, count)] = lax.dot_general(
                pick, rows, (((1,), (1,)), ((), ())), preferred_element_type=jnp.float32
            ).astype(jnp.bfloat16)

        for c in range(CORES):
            for page in range(0, P_DEV, 2):
                rows = v_stage[c, pl.ds(page, 2), :, window].reshape(2 * PAGE, WINDOW)
                place(rows, (c * P_DEV + page) * PAGE, 2 * PAGE)
        place(jnp.concatenate([nv_stage[c, :, window] for c in range(CORES)], axis=0), CACHED, FRESH)

    row = lax.broadcasted_iota(jnp.int32, (FRESH, QW), 0)
    lane = lax.broadcasted_iota(jnp.int32, (FRESH, QW), 1)
    tile_row = lax.broadcasted_iota(jnp.int32, (2, QCHIP), 0)

    def unit_of(u):
        h, t = u // Z, u % Z
        return h, (t + h // (HEADS_CORE - 1)) % Z

    def score_tiles(u, par):
        h, k = unit_of(u)
        g = (z + k) % Z
        queries = jnp.concatenate([q_t[h, g, 0], q_t[h, g, 1]], axis=1)
        top = [None]

        def rows_from(at):
            tile = jnp.dot(
                k_heads[h, pl.ds(at, KEYS // 2), :], queries, preferred_element_type=jnp.float32)
            if at > 0:
                key_pos = jnp.where(
                    row < TOK_DEV, perm[blk_of(z, y, 0)], perm[blk_of(z, y, 1)]
                ) * TOK_DEV + row % TOK_DEV
                query_blk = jnp.zeros((FRESH, QW), jnp.int32)
                for j in range(Y * CORES):
                    query_blk = jnp.where(lane // TOK_DEV == j, perm[g * Y * CORES + j], query_blk)
                seen = query_blk * TOK_DEV + lane % TOK_DEV >= key_pos
                tile = jnp.concatenate(
                    [tile[:CACHED - at], jnp.where(seen, tile[CACHED - at:], -1e30)], axis=0)
            scores[par][pl.ds(at, KEYS // 2), :] = tile
            tile_top = jnp.max(tile.reshape(KEYS // 16, 8, QW), axis=0)
            top[0] = tile_top if top[0] is None else jnp.maximum(top[0], tile_top)
            if at > 0:
                tops[par] = jnp.broadcast_to(
                    jnp.max(top[0], axis=0, keepdims=True) * LOG2_SCALE, (8, QW))

        steps = [lambda: None] * 9
        steps[1] = lambda: rows_from(0)
        steps[5] = lambda: rows_from(KEYS // 2)
        return steps

    def weight_tiles(par):
        top = tops[par][0:1]
        tops[2 + par] = tops[par]

        def weigh(at, count):
            tile = scores[par][pl.ds(at, count), :]
            probs[par][pl.ds(at, count), :] = jnp.exp2(tile * LOG2_SCALE - top).astype(jnp.bfloat16)

        spans = [(i * 256, 256) for i in range(CACHED // 256)] + [(CACHED, FRESH)]
        return [lambda s=s: weigh(*s) for s in spans]

    def value_tiles(u, par, numer):
        h, _ = unit_of(u)

        def add(at, count):
            term = jnp.dot(
                v_t[h, :, pl.ds(at, count)], probs[par][pl.ds(at, count), :],
                preferred_element_type=jnp.float32)
            numer[0] = term if numer[0] is None else numer[0] + term

        def nothing():
            pass

        steps = [nothing] * 9
        steps[0] = lambda: add(0, KEYS)
        return steps

    def merge(u):
        h, k = unit_of(u)
        g = (z + k) % Z
        for copy in reduce_y(h, g):
            copy.wait_recv()
        own, other = part_stat[h, g, y], y_stat[h, g]
        top = jnp.maximum(own[0:1], other[0:1])
        own_factor, other_factor = jnp.exp2(own[0:1] - top), jnp.exp2(other[0:1] - top)
        total = own[1:2] * own_factor + other[1:2] * other_factor
        numer = part[h, g, y] * own_factor + y_part[h, g].astype(jnp.float32) * other_factor
        z_src[h, g] = numer.astype(jnp.bfloat16)
        z_src_stat[h, g] = jnp.where(tile_row == 0, top, total)

        @pl.when(k > 0)
        def _():
            for copy in reduce_z(h, k):
                copy.start()

    def finish(h, send=None):
        for d in range(1, Z):
            for copy in reduce_z(h, d):
                copy.wait_recv()
        stats = [z_src_stat[h, z]] + [z_stat[h, d] for d in range(1, Z)]
        numers = [z_src[h, z]] + [z_part[h, d] for d in range(1, Z)]
        top = stats[0][0:1]
        for stat in stats[1:]:
            top = jnp.maximum(top, stat[0:1])
        total = jnp.zeros((1, QCHIP), jnp.float32)
        numer = jnp.zeros((HD, QCHIP), jnp.float32)
        for stat, term in zip(stats, numers):
            factor = jnp.exp2(stat[0:1] - top)
            total = total + stat[1:2] * factor
            numer = numer + term.astype(jnp.float32) * factor
        mixed = (numer / total).T.astype(jnp.bfloat16)
        w_rows = pl.ds(pl.multiple_of(h * HD, 32), HD)
        for place, half in enumerate((1 - x, x)):
            for part_index in range(2):
                for at, count in ((0, 512), (512, 384)):
                    w_cols = pl.ds(
                        pl.multiple_of(half * COLS + part_index * CHUNK + at, 128), count)
                    term = jnp.dot(mixed, w_all[w_rows, w_cols], preferred_element_type=jnp.float32)
                    for c in range(CORES):
                        acc[half, part_index, c, :, pl.ds(at, count)] += (
                            term[c * TOK_DEV:(c + 1) * TOK_DEV])
                if send is not None:
                    send(place, half, part_index)

    def step(u, par, score, weigh, value):
        lists = []
        numer = [None]
        old_top = tops[2 + par][0:1] if value else None
        if score:
            h, k = unit_of(u)
            d = (Z - k) % Z
            gather_y(h, d).wait_recv()

            @pl.when((k > 0) & (h < HEADS_CORE - 1))
            def _():
                forward(h + 1, d)

            @pl.when((k == 1) & (h < HEADS_CORE - 2))
            def _():
                send_queries(h + 2)

        if value:
            lists.append(value_tiles(u - 2, par, numer))
        if weigh:
            lists.append(weight_tiles(1 - par))
        if score:
            lists.append(score_tiles(u, par))
        for group in zip(*lists):
            for work in group:
                work()
        if value:
            h, k = unit_of(u - 2)
            g = (z + k) % Z
            for j in range(Y):
                cols = slice(j * QCHIP, (j + 1) * QCHIP)
                part[h, g, j] = numer[0][:HD, cols]
                part_16[h, g, j] = numer[0][:HD, cols].astype(jnp.bfloat16)
                part_stat[h, g, j] = jnp.where(
                    tile_row == 0, old_top[:, cols], numer[0][HD:HD + 1, cols])
            for copy in reduce_y(h, g):
                copy.start()

    def beside(u):
        @pl.when((u % Z == 2) & (u < UNITS - Z))
        def _():
            prepare_keys(u // Z + 1)
            prepare_values(u // Z + 1)

        @pl.when(u >= 2 + LAG)
        def _():
            merge(u - 2 - LAG)

        @pl.when((u >= 10) & (u % Z == 2))
        def _():
            finish((u - 10) // Z)

    arrived(1)
    arrived(2)
    prepare_keys(0)
    for d in range(1, Z):
        forward(0, d)
    send_queries(1)
    arrived(3)
    arrived(4)
    prepare_values(0)
    w_copy.wait()

    step(0, 0, True, False, False)
    step(1, 1, True, True, False)

    @pl.loop(1, UNITS // 2)
    def _(pair):
        for par in range(2):
            step(2 * pair + par, par, True, True, True)
            beside(2 * pair + par)

    step(UNITS, 0, False, True, True)
    merge(UNITS - 2 - LAG)
    step(UNITS + 1, 1, False, False, True)
    merge(UNITS - 1 - LAG)
    finish(HEADS_CORE - 2)
    for u in range(UNITS - LAG, UNITS):
        merge(u)

    core_out = {}

    def send_core(place, half, part_index):
        i = place * 2 + part_index
        core_out[i] = remote(
            acc.at[half, part_index, 1 - core], c_part.at[place, part_index],
            o_send.at[i], o_recv.at[i], sibling)
        core_out[i].start()

    finish(HEADS_CORE - 1, send_core)
    across = []
    for i in range(2):
        core_out[i].wait_recv()
        x_src[i] = (acc[1 - x, i, core] + c_part[0, i]).astype(jnp.bfloat16)
        copy = remote(x_src.at[i], x_part.at[i], o_send.at[4 + i], o_recv.at[4 + i], x_peer)
        copy.start()
        across.append(copy)
    for i in range(2):
        core_out[2 + i].wait_recv()
        c_part[1, i] = acc[x, i, core] + c_part[1, i]
    for i in range(2):
        across[i].wait_recv()
        out_ref[:, pl.ds(i * CHUNK, CHUNK)] = (
            c_part[1, i] + x_part[i].astype(jnp.float32)).astype(jnp.bfloat16)

    for copy in core_copies + list(core_out.values()) + across:
        copy.wait_send()

    @pl.loop(0, HEADS_CORE)
    def _(h):
        for d in range(Z):
            gather_y(h, d).wait_send()
            for copy in reduce_y(h, d):
                copy.wait_send()
            if d > 0:
                gather_z(h, d).wait_send()
                for copy in reduce_z(h, d):
                    copy.wait_send()


def fused_shards(
    queries, new_keys, new_values, key_cache, value_cache, out_weight,
    cache_len, page_table, block_perm,
):
    bf16, f32 = jnp.bfloat16, jnp.float32
    vmem, dma = pltpu.VMEM, pltpu.SemaphoreType.DMA
    hc = HEADS_CORE
    block = (HD, QCHIP)
    stat = (2, QCHIP)
    scratch = [
        vmem((CORES, TOK_DEV, GROUP), bf16),
        vmem((CORES, TOK_DEV, GROUP), bf16),
        vmem((CORES, TOK_DEV, GROUP), bf16),
        vmem((CORES, P_DEV, PAGE, GROUP), bf16),
        vmem((CORES, P_DEV, PAGE, GROUP), bf16),
        vmem((GROUP, XS * COLS), bf16),
        vmem((hc, Z, Y) + block, bf16),
        vmem((hc, KEYS, HD), bf16),
        vmem((hc, VROWS, KEYS), bf16),
        vmem((KEYS, QW), f32),
        vmem((KEYS, QW), f32),
        vmem((KEYS, QW), bf16),
        vmem((KEYS, QW), bf16),
        vmem((4, 8, QW), f32),
        vmem((hc, Z, Y) + block, f32),
        vmem((hc, Z, Y) + block, bf16),
        vmem((hc, Z, Y) + stat, f32),
        vmem((hc, Z) + block, bf16),
        vmem((hc, Z) + stat, f32),
        vmem((hc, Z) + block, bf16),
        vmem((hc, Z) + stat, f32),
        vmem((hc, Z) + block, bf16),
        vmem((hc, Z) + stat, f32),
        vmem((XS, 2, CORES, TOK_DEV, CHUNK), f32),
        vmem((2, 2, TOK_DEV, CHUNK), f32),
        vmem((2, TOK_DEV, CHUNK), bf16),
        vmem((2, TOK_DEV, CHUNK), bf16),
        dma((6,)), dma((5,)), dma((5,)),
        dma((hc, Z)), dma((hc, Z)), dma((hc, Z)), dma((hc, Z)),
        dma((hc, Z, 2)), dma((hc, Z, 2)), dma((hc, Z, 2)), dma((hc, Z, 2)),
        dma((6,)), dma((6,)),
    ]
    flops = 4 * hc * Z * QW * KEYS * HD + 2 * QCHIP * GROUP * XS * COLS
    return pl.pallas_call(
        fused_kernel,
        out_shape=jax.ShapeDtypeStruct((TOK_DEV, COLS), bf16),
        in_specs=[pl.BlockSpec(memory_space=pltpu.SMEM)] + [pl.BlockSpec(memory_space=pl.ANY)] * 6,
        out_specs=pl.BlockSpec(memory_space=pltpu.VMEM),
        scratch_shapes=scratch,
        compiler_params=pltpu.CompilerParams(
            collective_id=0, has_side_effects=True, vmem_limit_bytes=56 * 1024 * 1024),
        cost_estimate=pl.CostEstimate(
            flops=flops, bytes_accessed=14 * 1024 * 1024, transcendentals=hc * Z * QW * KEYS),
    )(block_perm, queries, new_keys, new_values, key_cache, value_cache, out_weight)


def solution(mesh):
    in_specs = (
        P("blk", "head"),
        P("blk", "head"),
        P("blk", "head"),
        P("blk", None, "head"),
        P("blk", None, "head"),
        P("head", None),
        P(),
        P(),
        P(),
    )
    out_specs = P("blk", "head")
    local = fused_shards if fits_fused(mesh) else shards
    return jax.shard_map(local, mesh=mesh, in_specs=in_specs, out_specs=out_specs, check_vma=False)
```

```python
import math

import jax
import jax.numpy as jnp
from jax import lax
from jax.experimental import pallas as pl
from jax.experimental.pallas import tpu as pltpu
from jax.sharding import PartitionSpec as P

HD = 224
PAGE = 128
P_DEV = 8
NEW = 1024
TOK_DEV = 64
MAXP = 128


def block_partial(query_rows, key_rows, value_rows, visible):
    head_count = query_rows.shape[1] // HD
    query_heads = query_rows.reshape(query_rows.shape[0], head_count, HD)
    key_heads = key_rows.reshape(key_rows.shape[0], head_count, HD)
    value_heads = value_rows.reshape(value_rows.shape[0], head_count, HD)
    scores = jnp.einsum(
        "qhd,khd->hqk", query_heads, key_heads, preferred_element_type=jnp.float32
    ) * (1.0 / math.sqrt(HD))
    scores = jnp.where(visible[None], scores, -1e30)
    row_top = jnp.max(scores, axis=2)
    weights = jnp.where(visible[None], jnp.exp(scores - row_top[:, :, None]), 0.0).astype(
        jnp.bfloat16
    )
    row_sum = jnp.sum(weights.astype(jnp.float32), axis=2)
    numerators = jnp.einsum(
        "hqk,khd->qhd", weights, value_heads, preferred_element_type=jnp.float32
    )
    return (row_top.T, row_sum.T, numerators)


def absorb(carry_state, request, partial_value):
    numer_all, top_all, sum_all = carry_state
    part_top, part_sum, part_numer = partial_value
    old_top = lax.dynamic_index_in_dim(top_all, request, 0, keepdims=False)
    old_sum = lax.dynamic_index_in_dim(sum_all, request, 0, keepdims=False)
    old_numer = lax.dynamic_index_in_dim(numer_all, request, 0, keepdims=False)
    new_top = jnp.maximum(old_top, part_top)
    old_factor = jnp.exp(old_top - new_top)
    part_factor = jnp.exp(part_top - new_top)
    merged_sum = old_factor * old_sum + part_factor * part_sum
    merged_numer = old_numer * old_factor[:, :, None] + part_numer * part_factor[:, :, None]
    return (
        lax.dynamic_update_index_in_dim(numer_all, merged_numer, request, 0),
        lax.dynamic_update_index_in_dim(top_all, new_top, request, 0),
        lax.dynamic_update_index_in_dim(sum_all, merged_sum, request, 0),
    )


def shards(
    queries,
    new_keys,
    new_values,
    key_cache,
    value_cache,
    out_weight,
    cache_len,
    page_table,
    block_perm,
):
    row_width = queries.shape[1]
    head_count = row_width // HD
    blk_count = lax.axis_size("blk")
    my_index = lax.axis_index("blk")
    req_count = cache_len.shape[0]
    blocks_per_req = NEW // TOK_DEV
    gathered = lax.all_gather(queries, "blk", axis=0, tiled=True)
    block_ids = jnp.arange(blk_count, dtype=jnp.int32)
    inverse = jnp.zeros((blk_count,), jnp.int32).at[block_perm].set(block_ids)
    query_all = gathered.reshape(blk_count, TOK_DEV, row_width)[inverse].reshape(
        req_count, NEW, row_width
    )
    global_ids = my_index * P_DEV + jnp.arange(P_DEV, dtype=jnp.int32)
    table_ids = jnp.arange(page_table.shape[0], dtype=jnp.int32)
    match_rows = page_table[None, :] == global_ids[:, None]
    logical = jnp.sum(jnp.where(match_rows, table_ids[None, :], 0), axis=1)
    page_req = logical // MAXP
    page_pos = logical % MAXP
    page_fill = jnp.clip(cache_len[page_req] - page_pos * PAGE, 0, PAGE)
    slot_ids = jnp.arange(PAGE, dtype=jnp.int32)
    start_state = (
        jnp.zeros((req_count, NEW, head_count, HD), jnp.float32),
        jnp.full((req_count, NEW, head_count), -1e30, jnp.float32),
        jnp.zeros((req_count, NEW, head_count), jnp.float32),
    )

    def page_work(slot_index, carry_state):
        request = page_req[slot_index]
        query_rows = lax.dynamic_index_in_dim(query_all, request, 0, keepdims=False)
        key_rows = lax.dynamic_index_in_dim(key_cache, slot_index, 0, keepdims=False)
        value_rows = lax.dynamic_index_in_dim(value_cache, slot_index, 0, keepdims=False)
        visible = jnp.broadcast_to((slot_ids < page_fill[slot_index])[None, :], (NEW, PAGE))
        return absorb(
            carry_state, request, block_partial(query_rows, key_rows, value_rows, visible)
        )

    def page_step(slot_index, carry_state):
        return page_work(slot_index, carry_state)

    carry_state = lax.fori_loop(0, P_DEV, page_step, start_state)
    my_block = block_perm[my_index]
    my_request = my_block // blocks_per_req
    my_offset = my_block % blocks_per_req * TOK_DEV
    new_pos = jnp.arange(NEW, dtype=jnp.int32)[:, None]
    key_pos = my_offset + jnp.arange(TOK_DEV, dtype=jnp.int32)[None, :]
    own_rows = lax.dynamic_index_in_dim(query_all, my_request, 0, keepdims=False)
    carry_state = absorb(
        carry_state, my_request, block_partial(own_rows, new_keys, new_values, new_pos >= key_pos)
    )
    numer_all, top_all, sum_all = carry_state
    send_numer = numer_all.reshape(blk_count, TOK_DEV, row_width)[block_perm]
    send_top = top_all.reshape(blk_count, TOK_DEV, head_count)[block_perm]
    send_sum = sum_all.reshape(blk_count, TOK_DEV, head_count)[block_perm]
    recv_numer, recv_top, recv_sum = (
        lax.all_to_all(send_numer, "blk", split_axis=0, concat_axis=0, tiled=True),
        lax.all_to_all(send_top, "blk", split_axis=0, concat_axis=0, tiled=True),
        lax.all_to_all(send_sum, "blk", split_axis=0, concat_axis=0, tiled=True),
    )
    best_top = jnp.max(recv_top, axis=0)
    factor = jnp.exp(recv_top - best_top[None])
    total_sum = jnp.sum(recv_sum * factor, axis=0)
    total_numer = jnp.sum(
        recv_numer.reshape(blk_count, TOK_DEV, head_count, HD) * factor[..., None], axis=0
    )
    mixed = (total_numer / total_sum[:, :, None]).reshape(TOK_DEV, row_width).astype(jnp.bfloat16)
    head_term = jnp.dot(mixed, out_weight, preferred_element_type=jnp.float32)
    return lax.psum_scatter(head_term, "head", scatter_dimension=1, tiled=True).astype(jnp.bfloat16)


MESH = pl.DeviceIdType.MESH
Z, Y, CORES, XS = 4, 2, 2, 2
HEADS_CORE = 4
GROUP = HEADS_CORE * HD
CACHED = CORES * P_DEV * PAGE
FRESH = CORES * TOK_DEV
KEYS = CACHED + FRESH
QCHIP = CORES * TOK_DEV
QW = Y * QCHIP
VROWS = HD + 16
COLS = 1792
CHUNK = COLS // 2
WINDOW = 384
UNITS = HEADS_CORE * Z
LAG = 2
LOG2_SCALE = math.log2(math.e) / math.sqrt(HD)


def fits_fused(mesh):
    return dict(mesh.shape) == {"blk": Z * Y * CORES, "head": XS}


def fused_kernel(
    perm, q_hbm, nk_hbm, nv_hbm, kc_hbm, vc_hbm, w_hbm, out_ref,
    q_stage, nk_stage, nv_stage, k_stage, v_stage, w_all,
    q_t, k_heads, v_t, scores_a, scores_b, probs_a, probs_b, tops,
    part, part_16, part_stat, y_part, y_stat,
    z_src, z_src_stat, z_part, z_stat,
    acc, c_part, x_src, x_part, w_far, w_near, mix_src, mix_in,
    local_sem, core_send, core_recv, gz_send, gz_recv, gy_send, gy_recv,
    ry_send, ry_recv, rz_send, rz_recv, o_send, o_recv, w_send, w_recv, m_send, m_recv,
):
    me = lax.axis_index("blk")
    x = lax.axis_index("head")
    core = me % CORES
    y = (me // CORES) % Y
    z = me // (CORES * Y)
    scores, probs = (scores_a, scores_b), (probs_a, probs_b)

    def blk_of(zz, yy, cc):
        return (zz * Y + yy) * CORES + cc

    sibling = (blk_of(z, y, 1 - core), x)
    y_peer = (blk_of(z, 1 - y, core), x)
    x_peer = (me, 1 - x)
    x_sibling = (blk_of(z, y, 1 - core), 1 - x)
    last = HEADS_CORE - 1

    def z_to(d):
        return (blk_of((z + d) % Z, y, core), x)

    def remote(src, dst, send_sem, recv_sem, peer):
        return pltpu.make_async_remote_copy(
            src_ref=src, dst_ref=dst, send_sem=send_sem, recv_sem=recv_sem,
            device_id=peer, device_id_type=MESH)

    barrier = pltpu.get_barrier_semaphore()
    peers = [sibling, y_peer, x_peer, x_sibling] + [z_to(d) for d in range(1, Z)]
    for peer in peers:
        pl.semaphore_signal(barrier, inc=1, device_id=peer, device_id_type=MESH)

    mine = pl.ds(pl.multiple_of(core * GROUP, 128), GROUP)
    theirs = pl.ds(pl.multiple_of((1 - core) * GROUP, 128), GROUP)
    staged = [
        (q_hbm, q_stage), (kc_hbm, k_stage), (nk_hbm, nk_stage),
        (vc_hbm, v_stage), (nv_hbm, nv_stage),
    ]
    local_copies, core_copies = [], []
    for i, (src, dst) in enumerate(staged):
        lead = (slice(None),) * (len(src.shape) - 1)
        copy = pltpu.make_async_copy(src.at[lead + (mine,)], dst.at[core], local_sem.at[i])
        copy.start()
        local_copies.append(copy)

    pl.semaphore_wait(barrier, len(peers))
    for i, (src, dst) in enumerate(staged):
        lead = (slice(None),) * (len(src.shape) - 1)
        copy = remote(
            src.at[lead + (theirs,)], dst.at[core], core_send.at[i], core_recv.at[i], sibling)
        copy.start()
        core_copies.append(copy)
    w_copy = pltpu.make_async_copy(
        w_hbm.at[pl.ds(pl.multiple_of(core * GROUP, 128), GROUP), :], w_all, local_sem.at[5])
    w_copy.start()
    near_row = pl.multiple_of((1 - core) * GROUP + last * HD, 32)
    near_copy = pltpu.make_async_copy(
        w_hbm.at[pl.ds(near_row, HD), pl.ds(pl.multiple_of(x * COLS, 128), COLS)],
        w_near, local_sem.at[6])
    near_copy.start()
    far_copies = []
    for c in range(CORES):
        copy = remote(
            w_hbm.at[pl.ds(c * GROUP + last * HD, HD),
                     pl.ds(pl.multiple_of((1 - x) * COLS, 128), COLS)],
            w_far.at[c], w_send.at[c], w_recv.at[c], x_peer)
        copy.start()
        far_copies.append(copy)

    def arrived(i):
        local_copies[i].wait()
        core_copies[i].wait_recv()

    def gather_z(h, d):
        block = q_t.at[h, z, y]
        return remote(block, block, gz_send.at[h, d], gz_recv.at[h, d], z_to(d))

    def gather_y(h, d):
        block = q_t.at[h, (z + Z - d) % Z, y]
        return remote(block, block, gy_send.at[h, d], gy_recv.at[h, d], y_peer)

    def forward(h, d):
        gather_z(h, d).wait_recv()
        gather_y(h, d).start()

    def reduce_y(h, g):
        return (
            remote(part_16.at[h, g, 1 - y], y_part.at[h, g],
                   ry_send.at[h, g, 0], ry_recv.at[h, g, 0], y_peer),
            remote(part_stat.at[h, g, 1 - y], y_stat.at[h, g],
                   ry_send.at[h, g, 1], ry_recv.at[h, g, 1], y_peer),
        )

    def reduce_z(h, d):
        to = (z + d) % Z
        return (
            remote(z_src.at[h, to], z_part.at[h, d],
                   rz_send.at[h, d, 0], rz_recv.at[h, d, 0], z_to(d)),
            remote(z_src_stat.at[h, to], z_stat.at[h, d],
                   rz_send.at[h, d, 1], rz_recv.at[h, d, 1], z_to(d)),
        )

    arrived(0)
    q_rows = jnp.concatenate([q_stage[0], q_stage[1]], axis=0).astype(jnp.float32)
    q_cols = q_rows.T.astype(jnp.bfloat16)
    for h in range(HEADS_CORE):
        q_t[h, z, y] = q_cols[h * HD:(h + 1) * HD]

    def send_queries(h):
        for d in range(1, Z):
            gather_z(h, d).start()
        gather_y(h, 0).start()

    send_queries(0)

    v_t[:, pl.ds(HD, VROWS - HD), :] = jnp.ones((HEADS_CORE, VROWS - HD, KEYS), jnp.bfloat16)
    acc[...] = jnp.zeros(acc.shape, jnp.float32)

    def head_window(h):
        start = jnp.minimum(h * HD // 128 * 128, GROUP - WINDOW)
        return pl.ds(pl.multiple_of(start, 128), WINDOW), h * HD - start

    def prepare_keys(h):
        window, offset = head_window(h)
        pick = jnp.where(
            lax.broadcasted_iota(jnp.int32, (WINDOW, HD), 0)
            == lax.broadcasted_iota(jnp.int32, (WINDOW, HD), 1) + offset, 1.0, 0.0
        ).astype(jnp.bfloat16)

        def place(rows, at, count):
            k_heads[h, pl.ds(at, count), :] = jnp.dot(
                rows, pick, preferred_element_type=jnp.float32).astype(jnp.bfloat16)

        for c in range(CORES):
            for page in range(0, P_DEV, 2):
                rows = k_stage[c, pl.ds(page, 2), :, window].reshape(2 * PAGE, WINDOW)
                place(rows, (c * P_DEV + page) * PAGE, 2 * PAGE)
            place(nk_stage[c, :, window], CACHED + c * TOK_DEV, TOK_DEV)

    def prepare_values(h):
        window, offset = head_window(h)
        pick = jnp.where(
            lax.broadcasted_iota(jnp.int32, (HD, WINDOW), 1)
            == lax.broadcasted_iota(jnp.int32, (HD, WINDOW), 0) + offset, 1.0, 0.0
        ).astype(jnp.bfloat16)

        def place(rows, at, count):
            v_t[h, pl.ds(0, HD), pl.ds(at, count)] = lax.dot_general(
                pick, rows, (((1,), (1,)), ((), ())), preferred_element_type=jnp.float32
            ).astype(jnp.bfloat16)

        for c in range(CORES):
            for page in range(0, P_DEV, 2):
                rows = v_stage[c, pl.ds(page, 2), :, window].reshape(2 * PAGE, WINDOW)
                place(rows, (c * P_DEV + page) * PAGE, 2 * PAGE)
        place(jnp.concatenate([nv_stage[c, :, window] for c in range(CORES)], axis=0), CACHED, FRESH)

    row = lax.broadcasted_iota(jnp.int32, (FRESH, QW), 0)
    lane = lax.broadcasted_iota(jnp.int32, (FRESH, QW), 1)
    tile_row = lax.broadcasted_iota(jnp.int32, (2, QCHIP), 0)

    def unit_of(u):
        h, t = u // Z, u % Z
        return h, (t + h // (HEADS_CORE - 1)) % Z

    def score_tiles(u, par):
        h, k = unit_of(u)
        g = (z + k) % Z
        queries = jnp.concatenate([q_t[h, g, 0], q_t[h, g, 1]], axis=1)
        top = [None]

        def rows_from(at):
            tile = jnp.dot(
                k_heads[h, pl.ds(at, KEYS // 2), :], queries, preferred_element_type=jnp.float32)
            if at > 0:
                key_pos = jnp.where(
                    row < TOK_DEV, perm[blk_of(z, y, 0)], perm[blk_of(z, y, 1)]
                ) * TOK_DEV + row % TOK_DEV
                query_blk = jnp.zeros((FRESH, QW), jnp.int32)
                for j in range(Y * CORES):
                    query_blk = jnp.where(lane // TOK_DEV == j, perm[g * Y * CORES + j], query_blk)
                seen = query_blk * TOK_DEV + lane % TOK_DEV >= key_pos
                tile = jnp.concatenate(
                    [tile[:CACHED - at], jnp.where(seen, tile[CACHED - at:], -1e30)], axis=0)
            scores[par][pl.ds(at, KEYS // 2), :] = tile
            tile_top = jnp.max(tile.reshape(KEYS // 16, 8, QW), axis=0)
            top[0] = tile_top if top[0] is None else jnp.maximum(top[0], tile_top)
            if at > 0:
                tops[par] = jnp.broadcast_to(
                    jnp.max(top[0], axis=0, keepdims=True) * LOG2_SCALE, (8, QW))

        steps = [lambda: None] * 9
        steps[1] = lambda: rows_from(0)
        steps[5] = lambda: rows_from(KEYS // 2)
        return steps

    def weight_tiles(par):
        top = tops[par][0:1]
        tops[2 + par] = tops[par]

        def weigh(at, count):
            tile = scores[par][pl.ds(at, count), :]
            probs[par][pl.ds(at, count), :] = jnp.exp2(tile * LOG2_SCALE - top).astype(jnp.bfloat16)

        spans = [(i * 256, 256) for i in range(CACHED // 256)] + [(CACHED, FRESH)]
        return [lambda s=s: weigh(*s) for s in spans]

    def value_tiles(u, par, numer):
        h, _ = unit_of(u)

        def add(at, count):
            term = jnp.dot(
                v_t[h, :, pl.ds(at, count)], probs[par][pl.ds(at, count), :],
                preferred_element_type=jnp.float32)
            numer[0] = term if numer[0] is None else numer[0] + term

        def nothing():
            pass

        steps = [nothing] * 9
        steps[0] = lambda: add(0, KEYS)
        return steps

    def merge(u):
        h, k = unit_of(u)
        g = (z + k) % Z
        for copy in reduce_y(h, g):
            copy.wait_recv()
        own, other = part_stat[h, g, y], y_stat[h, g]
        top = jnp.maximum(own[0:1], other[0:1])
        own_factor, other_factor = jnp.exp2(own[0:1] - top), jnp.exp2(other[0:1] - top)
        total = own[1:2] * own_factor + other[1:2] * other_factor
        numer = part[h, g, y] * own_factor + y_part[h, g].astype(jnp.float32) * other_factor
        z_src[h, g] = numer.astype(jnp.bfloat16)
        z_src_stat[h, g] = jnp.where(tile_row == 0, top, total)

        @pl.when(k > 0)
        def _():
            for copy in reduce_z(h, k):
                copy.start()

    def mix(h):
        for d in range(1, Z):
            for copy in reduce_z(h, d):
                copy.wait_recv()
        stats = [z_src_stat[h, z]] + [z_stat[h, d] for d in range(1, Z)]
        numers = [z_src[h, z]] + [z_part[h, d] for d in range(1, Z)]
        top = stats[0][0:1]
        for stat in stats[1:]:
            top = jnp.maximum(top, stat[0:1])
        total = jnp.zeros((1, QCHIP), jnp.float32)
        numer = jnp.zeros((HD, QCHIP), jnp.float32)
        for stat, term in zip(stats, numers):
            factor = jnp.exp2(stat[0:1] - top)
            total = total + stat[1:2] * factor
            numer = numer + term.astype(jnp.float32) * factor
        return (numer / total).T.astype(jnp.bfloat16)

    def finish(h, send=None):
        mixed = mix(h)
        w_rows = pl.ds(pl.multiple_of(h * HD, 32), HD)
        for place, half in enumerate((1 - x, x)):
            for part_index in range(2):
                for at, count in ((0, 512), (512, 384)):
                    w_cols = pl.ds(
                        pl.multiple_of(half * COLS + part_index * CHUNK + at, 128), count)
                    term = jnp.dot(mixed, w_all[w_rows, w_cols], preferred_element_type=jnp.float32)
                    for c in range(CORES):
                        acc[half, part_index, c, :, pl.ds(at, count)] += (
                            term[c * TOK_DEV:(c + 1) * TOK_DEV])
                if send is not None:
                    send(place, half, part_index)

    def step(u, par, score, weigh, value):
        lists = []
        numer = [None]
        old_top = tops[2 + par][0:1] if value else None
        if score:
            h, k = unit_of(u)
            d = (Z - k) % Z
            gather_y(h, d).wait_recv()

            @pl.when((k > 0) & (h < HEADS_CORE - 1))
            def _():
                forward(h + 1, d)

            @pl.when((k == 1) & (h < HEADS_CORE - 2))
            def _():
                send_queries(h + 2)

        if value:
            lists.append(value_tiles(u - 2, par, numer))
        if weigh:
            lists.append(weight_tiles(1 - par))
        if score:
            lists.append(score_tiles(u, par))
        for group in zip(*lists):
            for work in group:
                work()
        if value:
            h, k = unit_of(u - 2)
            g = (z + k) % Z
            for j in range(Y):
                cols = slice(j * QCHIP, (j + 1) * QCHIP)
                part[h, g, j] = numer[0][:HD, cols]
                part_16[h, g, j] = numer[0][:HD, cols].astype(jnp.bfloat16)
                part_stat[h, g, j] = jnp.where(
                    tile_row == 0, old_top[:, cols], numer[0][HD:HD + 1, cols])
            for copy in reduce_y(h, g):
                copy.start()

    def beside(u):
        @pl.when((u % Z == 2) & (u < UNITS - Z))
        def _():
            prepare_keys(u // Z + 1)
            prepare_values(u // Z + 1)

        @pl.when(u >= 2 + LAG)
        def _():
            merge(u - 2 - LAG)

        @pl.when((u >= 10) & (u % Z == 2))
        def _():
            finish((u - 10) // Z)

    arrived(1)
    arrived(2)
    prepare_keys(0)
    for d in range(1, Z):
        forward(0, d)
    send_queries(1)
    step(0, 0, True, False, False)
    step(1, 1, True, True, False)
    arrived(3)
    arrived(4)
    prepare_values(0)
    w_copy.wait()

    @pl.loop(1, UNITS // 2)
    def _(pair):
        for par in range(2):
            step(2 * pair + par, par, True, True, True)
            beside(2 * pair + par)

    step(UNITS, 0, False, True, True)
    merge(UNITS - 2 - LAG)
    step(UNITS + 1, 1, False, False, True)
    merge(UNITS - 1 - LAG)
    core_out = {}

    def send_core(place, half, part_index):
        i = place * 2 + part_index
        core_out[i] = remote(
            acc.at[half, part_index, 1 - core], c_part.at[place, part_index],
            o_send.at[i], o_recv.at[i], sibling)
        core_out[i].start()

    finish(last - 1, send_core)
    merge(UNITS - 2)
    across = []
    for i in range(2):
        core_out[i].wait_recv()
        x_src[i] = (acc[1 - x, i, core] + c_part[0, i]).astype(jnp.bfloat16)
        copy = remote(x_src.at[i], x_part.at[i], o_send.at[4 + i], o_recv.at[4 + i], x_peer)
        copy.start()
        across.append(copy)
    merge(UNITS - 1)
    for i in range(2):
        core_out[2 + i].wait_recv()
        c_part[1, i] = acc[x, i, core] + c_part[1, i]
    near_copy.wait()
    for copy in far_copies:
        copy.wait_recv()

    mixed = mix(last)
    for c in range(CORES):
        mix_src[c] = jnp.concatenate(
            [mixed[c * TOK_DEV:(c + 1) * TOK_DEV], jnp.zeros((TOK_DEV, 256 - HD), jnp.bfloat16)],
            axis=1)
    mix_copies = []
    for i, (rows, peer) in enumerate(((core, x_peer), (1 - core, x_sibling), (1 - core, sibling))):
        copy = remote(mix_src.at[rows], mix_in.at[i], m_send.at[i], m_recv.at[i], peer)
        copy.start()
        mix_copies.append(copy)

    spans = ((0, 512), (512, 384), (CHUNK, 512), (CHUNK + 512, 384))

    def add_rows(rows, weight_of):
        for at, count in spans:
            i, inner = at // CHUNK, at % CHUNK
            c_part[1, i, :, pl.ds(inner, count)] += jnp.dot(
                rows, weight_of(at, count), preferred_element_type=jnp.float32)

    def own_weight(at, count):
        cols = pl.ds(pl.multiple_of(x * COLS + at, 128), count)
        return w_all[pl.ds(last * HD, HD), cols]

    add_rows(mix_src[core][:, :HD], own_weight)
    for i in range(2):
        across[i].wait_recv()
        c_part[1, i] += x_part[i].astype(jnp.float32)
    mix_copies[2].wait_recv()
    add_rows(mix_in[2][:, :HD], lambda at, count: w_near[:, pl.ds(at, count)])
    mix_copies[0].wait_recv()
    mix_copies[1].wait_recv()
    for at, count in spans:
        i, inner = at // CHUNK, at % CHUNK
        same = jnp.dot(
            mix_in[0][:, :HD], w_far[core, :, pl.ds(at, count)],
            preferred_element_type=jnp.float32)
        other = jnp.dot(
            mix_in[1][:, :HD], w_far[1 - core, :, pl.ds(at, count)],
            preferred_element_type=jnp.float32)
        out_ref[:, pl.ds(at, count)] = (
            c_part[1, i, :, pl.ds(inner, count)] + same + other).astype(jnp.bfloat16)

    for copy in far_copies + mix_copies:
        copy.wait_send()
    for copy in core_copies + list(core_out.values()) + across:
        copy.wait_send()

    @pl.loop(0, HEADS_CORE)
    def _(h):
        for d in range(Z):
            gather_y(h, d).wait_send()
            for copy in reduce_y(h, d):
                copy.wait_send()
            if d > 0:
                gather_z(h, d).wait_send()
                for copy in reduce_z(h, d):
                    copy.wait_send()


def fused_shards(
    queries, new_keys, new_values, key_cache, value_cache, out_weight,
    cache_len, page_table, block_perm,
):
    bf16, f32 = jnp.bfloat16, jnp.float32
    vmem, dma = pltpu.VMEM, pltpu.SemaphoreType.DMA
    hc = HEADS_CORE
    block = (HD, QCHIP)
    stat = (2, QCHIP)
    scratch = [
        vmem((CORES, TOK_DEV, GROUP), bf16),
        vmem((CORES, TOK_DEV, GROUP), bf16),
        vmem((CORES, TOK_DEV, GROUP), bf16),
        vmem((CORES, P_DEV, PAGE, GROUP), bf16),
        vmem((CORES, P_DEV, PAGE, GROUP), bf16),
        vmem((GROUP, XS * COLS), bf16),
        vmem((hc, Z, Y) + block, bf16),
        vmem((hc, KEYS, HD), bf16),
        vmem((hc, VROWS, KEYS), bf16),
        vmem((KEYS, QW), f32),
        vmem((KEYS, QW), f32),
        vmem((KEYS, QW), bf16),
        vmem((KEYS, QW), bf16),
        vmem((4, 8, QW), f32),
        vmem((hc, Z, Y) + block, f32),
        vmem((hc, Z, Y) + block, bf16),
        vmem((hc, Z, Y) + stat, f32),
        vmem((hc, Z) + block, bf16),
        vmem((hc, Z) + stat, f32),
        vmem((hc, Z) + block, bf16),
        vmem((hc, Z) + stat, f32),
        vmem((hc, Z) + block, bf16),
        vmem((hc, Z) + stat, f32),
        vmem((XS, 2, CORES, TOK_DEV, CHUNK), f32),
        vmem((2, 2, TOK_DEV, CHUNK), f32),
        vmem((2, TOK_DEV, CHUNK), bf16),
        vmem((2, TOK_DEV, CHUNK), bf16),
        vmem((CORES, HD, COLS), bf16),
        vmem((HD, COLS), bf16),
        vmem((CORES, TOK_DEV, 256), bf16),
        vmem((3, TOK_DEV, 256), bf16),
        dma((7,)), dma((5,)), dma((5,)),
        dma((hc, Z)), dma((hc, Z)), dma((hc, Z)), dma((hc, Z)),
        dma((hc, Z, 2)), dma((hc, Z, 2)), dma((hc, Z, 2)), dma((hc, Z, 2)),
        dma((6,)), dma((6,)), dma((2,)), dma((2,)), dma((3,)), dma((3,)),
    ]
    flops = 4 * hc * Z * QW * KEYS * HD + 2 * QCHIP * GROUP * XS * COLS
    return pl.pallas_call(
        fused_kernel,
        out_shape=jax.ShapeDtypeStruct((TOK_DEV, COLS), bf16),
        in_specs=[pl.BlockSpec(memory_space=pltpu.SMEM)] + [pl.BlockSpec(memory_space=pl.ANY)] * 6,
        out_specs=pl.BlockSpec(memory_space=pltpu.VMEM),
        scratch_shapes=scratch,
        compiler_params=pltpu.CompilerParams(
            collective_id=0, has_side_effects=True, vmem_limit_bytes=56 * 1024 * 1024),
        cost_estimate=pl.CostEstimate(
            flops=flops, bytes_accessed=14 * 1024 * 1024, transcendentals=hc * Z * QW * KEYS),
    )(block_perm, queries, new_keys, new_values, key_cache, value_cache, out_weight)


def solution(mesh):
    in_specs = (
        P("blk", "head"),
        P("blk", "head"),
        P("blk", "head"),
        P("blk", None, "head"),
        P("blk", None, "head"),
        P("head", None),
        P(),
        P(),
        P(),
    )
    out_specs = P("blk", "head")
    local = fused_shards if fits_fused(mesh) else shards
    return jax.shard_map(local, mesh=mesh, in_specs=in_specs, out_specs=out_specs, check_vma=False)
```

```python
import math

import jax
import jax.numpy as jnp
from jax import lax
from jax.experimental import pallas as pl
from jax.experimental.pallas import tpu as pltpu
from jax.sharding import PartitionSpec as P

HD = 224
PAGE = 128
P_DEV = 8
NEW = 1024
TOK_DEV = 64
MAXP = 128


def block_partial(query_rows, key_rows, value_rows, visible):
    head_count = query_rows.shape[1] // HD
    query_heads = query_rows.reshape(query_rows.shape[0], head_count, HD)
    key_heads = key_rows.reshape(key_rows.shape[0], head_count, HD)
    value_heads = value_rows.reshape(value_rows.shape[0], head_count, HD)
    scores = jnp.einsum(
        "qhd,khd->hqk", query_heads, key_heads, preferred_element_type=jnp.float32
    ) * (1.0 / math.sqrt(HD))
    scores = jnp.where(visible[None], scores, -1e30)
    row_top = jnp.max(scores, axis=2)
    weights = jnp.where(visible[None], jnp.exp(scores - row_top[:, :, None]), 0.0).astype(
        jnp.bfloat16
    )
    row_sum = jnp.sum(weights.astype(jnp.float32), axis=2)
    numerators = jnp.einsum(
        "hqk,khd->qhd", weights, value_heads, preferred_element_type=jnp.float32
    )
    return (row_top.T, row_sum.T, numerators)


def absorb(carry_state, request, partial_value):
    numer_all, top_all, sum_all = carry_state
    part_top, part_sum, part_numer = partial_value
    old_top = lax.dynamic_index_in_dim(top_all, request, 0, keepdims=False)
    old_sum = lax.dynamic_index_in_dim(sum_all, request, 0, keepdims=False)
    old_numer = lax.dynamic_index_in_dim(numer_all, request, 0, keepdims=False)
    new_top = jnp.maximum(old_top, part_top)
    old_factor = jnp.exp(old_top - new_top)
    part_factor = jnp.exp(part_top - new_top)
    merged_sum = old_factor * old_sum + part_factor * part_sum
    merged_numer = old_numer * old_factor[:, :, None] + part_numer * part_factor[:, :, None]
    return (
        lax.dynamic_update_index_in_dim(numer_all, merged_numer, request, 0),
        lax.dynamic_update_index_in_dim(top_all, new_top, request, 0),
        lax.dynamic_update_index_in_dim(sum_all, merged_sum, request, 0),
    )


def shards(
    queries,
    new_keys,
    new_values,
    key_cache,
    value_cache,
    out_weight,
    cache_len,
    page_table,
    block_perm,
):
    row_width = queries.shape[1]
    head_count = row_width // HD
    blk_count = lax.axis_size("blk")
    my_index = lax.axis_index("blk")
    req_count = cache_len.shape[0]
    blocks_per_req = NEW // TOK_DEV
    gathered = lax.all_gather(queries, "blk", axis=0, tiled=True)
    block_ids = jnp.arange(blk_count, dtype=jnp.int32)
    inverse = jnp.zeros((blk_count,), jnp.int32).at[block_perm].set(block_ids)
    query_all = gathered.reshape(blk_count, TOK_DEV, row_width)[inverse].reshape(
        req_count, NEW, row_width
    )
    global_ids = my_index * P_DEV + jnp.arange(P_DEV, dtype=jnp.int32)
    table_ids = jnp.arange(page_table.shape[0], dtype=jnp.int32)
    match_rows = page_table[None, :] == global_ids[:, None]
    logical = jnp.sum(jnp.where(match_rows, table_ids[None, :], 0), axis=1)
    page_req = logical // MAXP
    page_pos = logical % MAXP
    page_fill = jnp.clip(cache_len[page_req] - page_pos * PAGE, 0, PAGE)
    slot_ids = jnp.arange(PAGE, dtype=jnp.int32)
    start_state = (
        jnp.zeros((req_count, NEW, head_count, HD), jnp.float32),
        jnp.full((req_count, NEW, head_count), -1e30, jnp.float32),
        jnp.zeros((req_count, NEW, head_count), jnp.float32),
    )

    def page_work(slot_index, carry_state):
        request = page_req[slot_index]
        query_rows = lax.dynamic_index_in_dim(query_all, request, 0, keepdims=False)
        key_rows = lax.dynamic_index_in_dim(key_cache, slot_index, 0, keepdims=False)
        value_rows = lax.dynamic_index_in_dim(value_cache, slot_index, 0, keepdims=False)
        visible = jnp.broadcast_to((slot_ids < page_fill[slot_index])[None, :], (NEW, PAGE))
        return absorb(
            carry_state, request, block_partial(query_rows, key_rows, value_rows, visible)
        )

    def page_step(slot_index, carry_state):
        return page_work(slot_index, carry_state)

    carry_state = lax.fori_loop(0, P_DEV, page_step, start_state)
    my_block = block_perm[my_index]
    my_request = my_block // blocks_per_req
    my_offset = my_block % blocks_per_req * TOK_DEV
    new_pos = jnp.arange(NEW, dtype=jnp.int32)[:, None]
    key_pos = my_offset + jnp.arange(TOK_DEV, dtype=jnp.int32)[None, :]
    own_rows = lax.dynamic_index_in_dim(query_all, my_request, 0, keepdims=False)
    carry_state = absorb(
        carry_state, my_request, block_partial(own_rows, new_keys, new_values, new_pos >= key_pos)
    )
    numer_all, top_all, sum_all = carry_state
    send_numer = numer_all.reshape(blk_count, TOK_DEV, row_width)[block_perm]
    send_top = top_all.reshape(blk_count, TOK_DEV, head_count)[block_perm]
    send_sum = sum_all.reshape(blk_count, TOK_DEV, head_count)[block_perm]
    recv_numer, recv_top, recv_sum = (
        lax.all_to_all(send_numer, "blk", split_axis=0, concat_axis=0, tiled=True),
        lax.all_to_all(send_top, "blk", split_axis=0, concat_axis=0, tiled=True),
        lax.all_to_all(send_sum, "blk", split_axis=0, concat_axis=0, tiled=True),
    )
    best_top = jnp.max(recv_top, axis=0)
    factor = jnp.exp(recv_top - best_top[None])
    total_sum = jnp.sum(recv_sum * factor, axis=0)
    total_numer = jnp.sum(
        recv_numer.reshape(blk_count, TOK_DEV, head_count, HD) * factor[..., None], axis=0
    )
    mixed = (total_numer / total_sum[:, :, None]).reshape(TOK_DEV, row_width).astype(jnp.bfloat16)
    head_term = jnp.dot(mixed, out_weight, preferred_element_type=jnp.float32)
    return lax.psum_scatter(head_term, "head", scatter_dimension=1, tiled=True).astype(jnp.bfloat16)


MESH = pl.DeviceIdType.MESH
Z, Y, CORES, XS = 4, 2, 2, 2
HEADS_CORE = 4
GROUP = HEADS_CORE * HD
CACHED = CORES * P_DEV * PAGE
FRESH = CORES * TOK_DEV
KEYS = CACHED + FRESH
QCHIP = CORES * TOK_DEV
QW = Y * QCHIP
VROWS = HD + 16
COLS = 1792
CHUNK = COLS // 2
WINDOW = 384
UNITS = HEADS_CORE * Z
LAG = 3
CUTS = ((0, 256), (256, 256), (512, 256), (768, 128))
LOG2_SCALE = math.log2(math.e) / math.sqrt(HD)


def fits_fused(mesh):
    return dict(mesh.shape) == {"blk": Z * Y * CORES, "head": XS}


def fused_kernel(
    perm, q_hbm, nk_hbm, nv_hbm, kc_hbm, vc_hbm, w_hbm, out_ref,
    q_stage, nk_stage, nv_stage, k_stage, v_stage, w_all,
    q_t, k_heads, v_t, scores_a, scores_b, probs_a, probs_b, tops,
    part, part_16, part_stat, y_part, y_stat,
    z_src, z_src_stat, z_part, z_stat,
    acc, c_part, x_src, x_part, w_far, w_near, mix_src, mix_in,
    local_sem, core_send, core_recv, gz_send, gz_recv, gy_send, gy_recv,
    ry_send, ry_recv, rz_send, rz_recv, o_send, o_recv, w_send, w_recv, m_send, m_recv,
):
    me = lax.axis_index("blk")
    x = lax.axis_index("head")
    core = me % CORES
    y = (me // CORES) % Y
    z = me // (CORES * Y)
    scores, probs = (scores_a, scores_b), (probs_a, probs_b)

    def blk_of(zz, yy, cc):
        return (zz * Y + yy) * CORES + cc

    sibling = (blk_of(z, y, 1 - core), x)
    y_peer = (blk_of(z, 1 - y, core), x)
    x_peer = (me, 1 - x)
    x_sibling = (blk_of(z, y, 1 - core), 1 - x)
    last = HEADS_CORE - 1

    def z_to(d):
        return (blk_of((z + d) % Z, y, core), x)

    def remote(src, dst, send_sem, recv_sem, peer):
        return pltpu.make_async_remote_copy(
            src_ref=src, dst_ref=dst, send_sem=send_sem, recv_sem=recv_sem,
            device_id=peer, device_id_type=MESH)

    barrier = pltpu.get_barrier_semaphore()
    peers = [sibling, y_peer, x_peer, x_sibling] + [z_to(d) for d in range(1, Z)]
    for peer in peers:
        pl.semaphore_signal(barrier, inc=1, device_id=peer, device_id_type=MESH)

    staged = {"q": (q_hbm, q_stage), "nk": (nk_hbm, nk_stage), "nv": (nv_hbm, nv_stage)}
    swaps = {}

    def swap(name, src, dst, i, at, count):
        lead = (slice(None),) * (len(src.shape) - 1)

        def cut(start):
            return pl.ds(pl.multiple_of(start * GROUP + at, 128), count)

        here = dst.at[(core,) + lead + (pl.ds(at, count),)]
        swaps[name] = (
            pltpu.make_async_copy(src.at[lead + (cut(core),)], here, local_sem.at[i]),
            remote(src.at[lead + (cut(1 - core),)], here, core_send.at[i], core_recv.at[i], sibling),
        )

    for i, (name, (src, dst)) in enumerate(staged.items()):
        swap(name, src, dst, i, 0, GROUP)
    for i, (at, count) in enumerate(CUTS):
        swap("k%d" % i, kc_hbm, k_stage, 3 + 2 * i, at, count)
        swap("v%d" % i, vc_hbm, v_stage, 4 + 2 * i, at, count)
    for name in ("q", "k0", "nk", "v0", "nv"):
        swaps[name][0].start()

    pl.semaphore_wait(barrier, len(peers))
    for name in ("q", "k0", "nk", "v0", "nv"):
        swaps[name][1].start()

    def start_swap(*names):
        for name in names:
            for copy in swaps[name]:
                copy.start()

    w_copy = pltpu.make_async_copy(
        w_hbm.at[pl.ds(pl.multiple_of(core * GROUP, 128), GROUP), :], w_all, local_sem.at[11])
    near_row = pl.multiple_of((1 - core) * GROUP + last * HD, 32)
    near_copy = pltpu.make_async_copy(
        w_hbm.at[pl.ds(near_row, HD), pl.ds(pl.multiple_of(x * COLS, 128), COLS)],
        w_near, local_sem.at[12])
    far_copies = []
    for c in range(CORES):
        copy = remote(
            w_hbm.at[pl.ds(c * GROUP + last * HD, HD),
                     pl.ds(pl.multiple_of((1 - x) * COLS, 128), COLS)],
            w_far.at[c], w_send.at[c], w_recv.at[c], x_peer)
        far_copies.append(copy)

    def arrived(*names):
        for name in names:
            swaps[name][0].wait()
            swaps[name][1].wait_recv()

    def gather_z(h, d):
        block = q_t.at[h, z, y]
        return remote(block, block, gz_send.at[h, d], gz_recv.at[h, d], z_to(d))

    def gather_y(h, d):
        block = q_t.at[h, (z + Z - d) % Z, y]
        return remote(block, block, gy_send.at[h, d], gy_recv.at[h, d], y_peer)

    def forward(h, d):
        gather_z(h, d).wait_recv()
        gather_y(h, d).start()

    def reduce_y(h, g):
        return (
            remote(part_16.at[h, g, 1 - y], y_part.at[h, g],
                   ry_send.at[h, g, 0], ry_recv.at[h, g, 0], y_peer),
            remote(part_stat.at[h, g, 1 - y], y_stat.at[h, g],
                   ry_send.at[h, g, 1], ry_recv.at[h, g, 1], y_peer),
        )

    def reduce_z(h, d):
        to = (z + d) % Z
        return (
            remote(z_src.at[h, to], z_part.at[h, d],
                   rz_send.at[h, d, 0], rz_recv.at[h, d, 0], z_to(d)),
            remote(z_src_stat.at[h, to], z_stat.at[h, d],
                   rz_send.at[h, d, 1], rz_recv.at[h, d, 1], z_to(d)),
        )

    arrived("q")
    q_rows = jnp.concatenate([q_stage[0], q_stage[1]], axis=0).astype(jnp.float32)
    q_cols = q_rows.T.astype(jnp.bfloat16)
    for h in range(HEADS_CORE):
        q_t[h, z, y] = q_cols[h * HD:(h + 1) * HD]

    def send_queries(h):
        for d in range(1, Z):
            gather_z(h, d).start()
        gather_y(h, 0).start()

    send_queries(0)

    v_t[:, pl.ds(HD, VROWS - HD), :] = jnp.ones((HEADS_CORE, VROWS - HD, KEYS), jnp.bfloat16)
    acc[...] = jnp.zeros(acc.shape, jnp.float32)

    def head_window(h):
        if isinstance(h, int) and h == 0:
            return pl.ds(0, 256), 0, 256
        start = jnp.minimum(h * HD // 128 * 128, GROUP - WINDOW)
        return pl.ds(pl.multiple_of(start, 128), WINDOW), h * HD - start, WINDOW

    def prepare_keys(h):
        window, offset, width = head_window(h)
        pick = jnp.where(
            lax.broadcasted_iota(jnp.int32, (width, HD), 0)
            == lax.broadcasted_iota(jnp.int32, (width, HD), 1) + offset, 1.0, 0.0
        ).astype(jnp.bfloat16)

        def place(rows, at, count):
            k_heads[h, pl.ds(at, count), :] = jnp.dot(
                rows, pick, preferred_element_type=jnp.float32).astype(jnp.bfloat16)

        for c in range(CORES):
            for page in range(0, P_DEV, 2):
                rows = k_stage[c, pl.ds(page, 2), :, window].reshape(2 * PAGE, width)
                place(rows, (c * P_DEV + page) * PAGE, 2 * PAGE)
            place(nk_stage[c, :, window], CACHED + c * TOK_DEV, TOK_DEV)

    def prepare_values(h):
        window, offset, width = head_window(h)
        pick = jnp.where(
            lax.broadcasted_iota(jnp.int32, (HD, width), 1)
            == lax.broadcasted_iota(jnp.int32, (HD, width), 0) + offset, 1.0, 0.0
        ).astype(jnp.bfloat16)

        def place(rows, at, count):
            v_t[h, pl.ds(0, HD), pl.ds(at, count)] = lax.dot_general(
                pick, rows, (((1,), (1,)), ((), ())), preferred_element_type=jnp.float32
            ).astype(jnp.bfloat16)

        for c in range(CORES):
            for page in range(0, P_DEV, 2):
                rows = v_stage[c, pl.ds(page, 2), :, window].reshape(2 * PAGE, width)
                place(rows, (c * P_DEV + page) * PAGE, 2 * PAGE)
        place(jnp.concatenate([nv_stage[c, :, window] for c in range(CORES)], axis=0), CACHED, FRESH)

    row = lax.broadcasted_iota(jnp.int32, (FRESH, QW), 0)
    lane = lax.broadcasted_iota(jnp.int32, (FRESH, QW), 1)
    tile_row = lax.broadcasted_iota(jnp.int32, (2, QCHIP), 0)

    def unit_of(u):
        h, t = u // Z, u % Z
        return h, (t + h // (HEADS_CORE - 1)) % Z

    def score_tiles(u, par):
        h, k = unit_of(u)
        g = (z + k) % Z
        queries = jnp.concatenate([q_t[h, g, 0], q_t[h, g, 1]], axis=1)
        top = [None]

        def rows_from(at):
            tile = jnp.dot(
                k_heads[h, pl.ds(at, KEYS // 2), :], queries, preferred_element_type=jnp.float32)
            if at > 0:
                key_pos = jnp.where(
                    row < TOK_DEV, perm[blk_of(z, y, 0)], perm[blk_of(z, y, 1)]
                ) * TOK_DEV + row % TOK_DEV
                query_blk = jnp.zeros((FRESH, QW), jnp.int32)
                for j in range(Y * CORES):
                    query_blk = jnp.where(lane // TOK_DEV == j, perm[g * Y * CORES + j], query_blk)
                seen = query_blk * TOK_DEV + lane % TOK_DEV >= key_pos
                tile = jnp.concatenate(
                    [tile[:CACHED - at], jnp.where(seen, tile[CACHED - at:], -1e30)], axis=0)
            scores[par][pl.ds(at, KEYS // 2), :] = tile
            tile_top = jnp.max(tile.reshape(KEYS // 16, 8, QW), axis=0)
            top[0] = tile_top if top[0] is None else jnp.maximum(top[0], tile_top)
            if at > 0:
                tops[par] = jnp.broadcast_to(
                    jnp.max(top[0], axis=0, keepdims=True) * LOG2_SCALE, (8, QW))

        steps = [lambda: None] * 9
        steps[1] = lambda: rows_from(0)
        steps[5] = lambda: rows_from(KEYS // 2)
        return steps

    def weight_tiles(par):
        top = tops[par][0:1]
        tops[2 + par] = tops[par]

        def weigh(at, count):
            tile = scores[par][pl.ds(at, count), :]
            probs[par][pl.ds(at, count), :] = jnp.exp2(tile * LOG2_SCALE - top).astype(jnp.bfloat16)

        spans = [(i * 256, 256) for i in range(CACHED // 256)] + [(CACHED, FRESH)]
        return [lambda s=s: weigh(*s) for s in spans]

    def value_tiles(u, par, numer):
        h, _ = unit_of(u)

        def add(at, count):
            term = jnp.dot(
                v_t[h, :, pl.ds(at, count)], probs[par][pl.ds(at, count), :],
                preferred_element_type=jnp.float32)
            numer[0] = term if numer[0] is None else numer[0] + term

        def nothing():
            pass

        steps = [nothing] * 9
        steps[0] = lambda: add(0, KEYS)
        return steps

    def merge(u):
        h, k = unit_of(u)
        g = (z + k) % Z
        for copy in reduce_y(h, g):
            copy.wait_recv()
        own, other = part_stat[h, g, y], y_stat[h, g]
        top = jnp.maximum(own[0:1], other[0:1])
        own_factor, other_factor = jnp.exp2(own[0:1] - top), jnp.exp2(other[0:1] - top)
        total = own[1:2] * own_factor + other[1:2] * other_factor
        numer = part[h, g, y] * own_factor + y_part[h, g].astype(jnp.float32) * other_factor
        z_src[h, g] = numer.astype(jnp.bfloat16)
        z_src_stat[h, g] = jnp.where(tile_row == 0, top, total)

        @pl.when(k > 0)
        def _():
            for copy in reduce_z(h, k):
                copy.start()

    def mix(h):
        for d in range(1, Z):
            for copy in reduce_z(h, d):
                copy.wait_recv()
        stats = [z_src_stat[h, z]] + [z_stat[h, d] for d in range(1, Z)]
        numers = [z_src[h, z]] + [z_part[h, d] for d in range(1, Z)]
        top = stats[0][0:1]
        for stat in stats[1:]:
            top = jnp.maximum(top, stat[0:1])
        total = jnp.zeros((1, QCHIP), jnp.float32)
        numer = jnp.zeros((HD, QCHIP), jnp.float32)
        for stat, term in zip(stats, numers):
            factor = jnp.exp2(stat[0:1] - top)
            total = total + stat[1:2] * factor
            numer = numer + term.astype(jnp.float32) * factor
        return (numer / total).T.astype(jnp.bfloat16)

    def finish(h, send=None):
        mixed = mix(h)
        w_rows = pl.ds(pl.multiple_of(h * HD, 32), HD)
        for place, half in enumerate((1 - x, x)):
            for part_index in range(2):
                for at, count in ((0, 512), (512, 384)):
                    w_cols = pl.ds(
                        pl.multiple_of(half * COLS + part_index * CHUNK + at, 128), count)
                    term = jnp.dot(mixed, w_all[w_rows, w_cols], preferred_element_type=jnp.float32)
                    for c in range(CORES):
                        acc[half, part_index, c, :, pl.ds(at, count)] += (
                            term[c * TOK_DEV:(c + 1) * TOK_DEV])
                if send is not None:
                    send(place, half, part_index)

    def step(u, par, score, weigh, value):
        lists = []
        numer = [None]
        old_top = tops[2 + par][0:1] if value else None
        if score:
            h, k = unit_of(u)
            d = (Z - k) % Z
            gather_y(h, d).wait_recv()

            @pl.when((k > 0) & (h < HEADS_CORE - 1))
            def _():
                forward(h + 1, d)

            @pl.when((k == 1) & (h < HEADS_CORE - 2))
            def _():
                send_queries(h + 2)

        if value:
            lists.append(value_tiles(u - 2, par, numer))
        if weigh:
            lists.append(weight_tiles(1 - par))
        if score:
            lists.append(score_tiles(u, par))
        for group in zip(*lists):
            for work in group:
                work()
        if value:
            h, k = unit_of(u - 2)
            g = (z + k) % Z
            for j in range(Y):
                cols = slice(j * QCHIP, (j + 1) * QCHIP)
                part[h, g, j] = numer[0][:HD, cols]
                part_16[h, g, j] = numer[0][:HD, cols].astype(jnp.bfloat16)
                part_stat[h, g, j] = jnp.where(
                    tile_row == 0, old_top[:, cols], numer[0][HD:HD + 1, cols])
            for copy in reduce_y(h, g):
                copy.start()

    def beside(u):
        for i in range(1, HEADS_CORE):
            @pl.when(u == i * Z - 2)
            def _():
                arrived("k%d" % i, "v%d" % i)

        @pl.when((u % Z == 2) & (u < UNITS - Z))
        def _():
            prepare_keys(u // Z + 1)
            prepare_values(u // Z + 1)

        @pl.when(u >= 2 + LAG)
        def _():
            merge(u - 2 - LAG)

        @pl.when(u == 9)
        def _():
            w_copy.wait()

        @pl.when((u >= 10) & (u % Z == 2))
        def _():
            finish((u - 10) // Z)

    arrived("k0", "nk")
    prepare_keys(0)
    for d in range(1, Z):
        forward(0, d)
    send_queries(1)
    start_swap("k1", "v1")
    step(0, 0, True, False, False)
    step(1, 1, True, True, False)
    arrived("v0", "nv")
    prepare_values(0)
    w_copy.start()
    start_swap("k2", "v2", "k3", "v3")
    near_copy.start()
    for copy in far_copies:
        copy.start()

    @pl.loop(1, UNITS // 2)
    def _(pair):
        for par in range(2):
            step(2 * pair + par, par, True, True, True)
            beside(2 * pair + par)

    step(UNITS, 0, False, True, True)
    merge(UNITS - 2 - LAG)
    step(UNITS + 1, 1, False, False, True)
    merge(UNITS - 1 - LAG)
    core_out = {}

    def send_core(place, half, part_index):
        i = place * 2 + part_index
        core_out[i] = remote(
            acc.at[half, part_index, 1 - core], c_part.at[place, part_index],
            o_send.at[i], o_recv.at[i], sibling)
        core_out[i].start()

    merge(UNITS - 3)
    finish(last - 1, send_core)
    merge(UNITS - 2)
    across = []
    for i in range(2):
        core_out[i].wait_recv()
        x_src[i] = (acc[1 - x, i, core] + c_part[0, i]).astype(jnp.bfloat16)
        copy = remote(x_src.at[i], x_part.at[i], o_send.at[4 + i], o_recv.at[4 + i], x_peer)
        copy.start()
        across.append(copy)
    merge(UNITS - 1)
    for i in range(2):
        core_out[2 + i].wait_recv()
        c_part[1, i] = acc[x, i, core] + c_part[1, i]
    near_copy.wait()
    for copy in far_copies:
        copy.wait_recv()

    mixed = mix(last)
    for c in range(CORES):
        mix_src[c] = jnp.concatenate(
            [mixed[c * TOK_DEV:(c + 1) * TOK_DEV], jnp.zeros((TOK_DEV, 256 - HD), jnp.bfloat16)],
            axis=1)
    mix_copies = []
    for i, (rows, peer) in enumerate(((core, x_peer), (1 - core, x_sibling), (1 - core, sibling))):
        copy = remote(mix_src.at[rows], mix_in.at[i], m_send.at[i], m_recv.at[i], peer)
        copy.start()
        mix_copies.append(copy)

    spans = ((0, 512), (512, 384), (CHUNK, 512), (CHUNK + 512, 384))

    def add_rows(rows, weight_of):
        for at, count in spans:
            i, inner = at // CHUNK, at % CHUNK
            c_part[1, i, :, pl.ds(inner, count)] += jnp.dot(
                rows, weight_of(at, count), preferred_element_type=jnp.float32)

    def own_weight(at, count):
        cols = pl.ds(pl.multiple_of(x * COLS + at, 128), count)
        return w_all[pl.ds(last * HD, HD), cols]

    add_rows(mix_src[core][:, :HD], own_weight)
    for i in range(2):
        across[i].wait_recv()
        c_part[1, i] += x_part[i].astype(jnp.float32)
    mix_copies[2].wait_recv()
    add_rows(mix_in[2][:, :HD], lambda at, count: w_near[:, pl.ds(at, count)])
    mix_copies[0].wait_recv()
    mix_copies[1].wait_recv()
    for at, count in spans:
        i, inner = at // CHUNK, at % CHUNK
        same = jnp.dot(
            mix_in[0][:, :HD], w_far[core, :, pl.ds(at, count)],
            preferred_element_type=jnp.float32)
        other = jnp.dot(
            mix_in[1][:, :HD], w_far[1 - core, :, pl.ds(at, count)],
            preferred_element_type=jnp.float32)
        out_ref[:, pl.ds(at, count)] = (
            c_part[1, i, :, pl.ds(inner, count)] + same + other).astype(jnp.bfloat16)

    for copy in far_copies + mix_copies:
        copy.wait_send()
    for copy in [pair[1] for pair in swaps.values()] + list(core_out.values()) + across:
        copy.wait_send()

    @pl.loop(0, HEADS_CORE)
    def _(h):
        for d in range(Z):
            gather_y(h, d).wait_send()
            for copy in reduce_y(h, d):
                copy.wait_send()
            if d > 0:
                gather_z(h, d).wait_send()
                for copy in reduce_z(h, d):
                    copy.wait_send()


def fused_shards(
    queries, new_keys, new_values, key_cache, value_cache, out_weight,
    cache_len, page_table, block_perm,
):
    bf16, f32 = jnp.bfloat16, jnp.float32
    vmem, dma = pltpu.VMEM, pltpu.SemaphoreType.DMA
    hc = HEADS_CORE
    block = (HD, QCHIP)
    stat = (2, QCHIP)
    scratch = [
        vmem((CORES, TOK_DEV, GROUP), bf16),
        vmem((CORES, TOK_DEV, GROUP), bf16),
        vmem((CORES, TOK_DEV, GROUP), bf16),
        vmem((CORES, P_DEV, PAGE, GROUP), bf16),
        vmem((CORES, P_DEV, PAGE, GROUP), bf16),
        vmem((GROUP, XS * COLS), bf16),
        vmem((hc, Z, Y) + block, bf16),
        vmem((hc, KEYS, HD), bf16),
        vmem((hc, VROWS, KEYS), bf16),
        vmem((KEYS, QW), f32),
        vmem((KEYS, QW), f32),
        vmem((KEYS, QW), bf16),
        vmem((KEYS, QW), bf16),
        vmem((4, 8, QW), f32),
        vmem((hc, Z, Y) + block, f32),
        vmem((hc, Z, Y) + block, bf16),
        vmem((hc, Z, Y) + stat, f32),
        vmem((hc, Z) + block, bf16),
        vmem((hc, Z) + stat, f32),
        vmem((hc, Z) + block, bf16),
        vmem((hc, Z) + stat, f32),
        vmem((hc, Z) + block, bf16),
        vmem((hc, Z) + stat, f32),
        vmem((XS, 2, CORES, TOK_DEV, CHUNK), f32),
        vmem((2, 2, TOK_DEV, CHUNK), f32),
        vmem((2, TOK_DEV, CHUNK), bf16),
        vmem((2, TOK_DEV, CHUNK), bf16),
        vmem((CORES, HD, COLS), bf16),
        vmem((HD, COLS), bf16),
        vmem((CORES, TOK_DEV, 256), bf16),
        vmem((3, TOK_DEV, 256), bf16),
        dma((13,)), dma((11,)), dma((11,)),
        dma((hc, Z)), dma((hc, Z)), dma((hc, Z)), dma((hc, Z)),
        dma((hc, Z, 2)), dma((hc, Z, 2)), dma((hc, Z, 2)), dma((hc, Z, 2)),
        dma((6,)), dma((6,)), dma((2,)), dma((2,)), dma((3,)), dma((3,)),
    ]
    flops = 4 * hc * Z * QW * KEYS * HD + 2 * QCHIP * GROUP * XS * COLS
    return pl.pallas_call(
        fused_kernel,
        out_shape=jax.ShapeDtypeStruct((TOK_DEV, COLS), bf16),
        in_specs=[pl.BlockSpec(memory_space=pltpu.SMEM)] + [pl.BlockSpec(memory_space=pl.ANY)] * 6,
        out_specs=pl.BlockSpec(memory_space=pltpu.VMEM),
        scratch_shapes=scratch,
        compiler_params=pltpu.CompilerParams(
            collective_id=0, has_side_effects=True, vmem_limit_bytes=56 * 1024 * 1024),
        cost_estimate=pl.CostEstimate(
            flops=flops, bytes_accessed=14 * 1024 * 1024, transcendentals=hc * Z * QW * KEYS),
    )(block_perm, queries, new_keys, new_values, key_cache, value_cache, out_weight)


def solution(mesh):
    in_specs = (
        P("blk", "head"),
        P("blk", "head"),
        P("blk", "head"),
        P("blk", None, "head"),
        P("blk", None, "head"),
        P("head", None),
        P(),
        P(),
        P(),
    )
    out_specs = P("blk", "head")
    local = fused_shards if fits_fused(mesh) else shards
    return jax.shard_map(local, mesh=mesh, in_specs=in_specs, out_specs=out_specs, check_vma=False)
```

```python
import math

import jax
import jax.numpy as jnp
from jax import lax
from jax.experimental import pallas as pl
from jax.experimental.pallas import tpu as pltpu
from jax.sharding import PartitionSpec as P

HD = 224
PAGE = 128
P_DEV = 8
NEW = 1024
TOK_DEV = 64
MAXP = 128


def block_partial(query_rows, key_rows, value_rows, visible):
    head_count = query_rows.shape[1] // HD
    query_heads = query_rows.reshape(query_rows.shape[0], head_count, HD)
    key_heads = key_rows.reshape(key_rows.shape[0], head_count, HD)
    value_heads = value_rows.reshape(value_rows.shape[0], head_count, HD)
    scores = jnp.einsum(
        "qhd,khd->hqk", query_heads, key_heads, preferred_element_type=jnp.float32
    ) * (1.0 / math.sqrt(HD))
    scores = jnp.where(visible[None], scores, -1e30)
    row_top = jnp.max(scores, axis=2)
    weights = jnp.where(visible[None], jnp.exp(scores - row_top[:, :, None]), 0.0).astype(
        jnp.bfloat16
    )
    row_sum = jnp.sum(weights.astype(jnp.float32), axis=2)
    numerators = jnp.einsum(
        "hqk,khd->qhd", weights, value_heads, preferred_element_type=jnp.float32
    )
    return (row_top.T, row_sum.T, numerators)


def absorb(carry_state, request, partial_value):
    numer_all, top_all, sum_all = carry_state
    part_top, part_sum, part_numer = partial_value
    old_top = lax.dynamic_index_in_dim(top_all, request, 0, keepdims=False)
    old_sum = lax.dynamic_index_in_dim(sum_all, request, 0, keepdims=False)
    old_numer = lax.dynamic_index_in_dim(numer_all, request, 0, keepdims=False)
    new_top = jnp.maximum(old_top, part_top)
    old_factor = jnp.exp(old_top - new_top)
    part_factor = jnp.exp(part_top - new_top)
    merged_sum = old_factor * old_sum + part_factor * part_sum
    merged_numer = old_numer * old_factor[:, :, None] + part_numer * part_factor[:, :, None]
    return (
        lax.dynamic_update_index_in_dim(numer_all, merged_numer, request, 0),
        lax.dynamic_update_index_in_dim(top_all, new_top, request, 0),
        lax.dynamic_update_index_in_dim(sum_all, merged_sum, request, 0),
    )


def shards(
    queries,
    new_keys,
    new_values,
    key_cache,
    value_cache,
    out_weight,
    cache_len,
    page_table,
    block_perm,
):
    row_width = queries.shape[1]
    head_count = row_width // HD
    blk_count = lax.axis_size("blk")
    my_index = lax.axis_index("blk")
    req_count = cache_len.shape[0]
    blocks_per_req = NEW // TOK_DEV
    gathered = lax.all_gather(queries, "blk", axis=0, tiled=True)
    block_ids = jnp.arange(blk_count, dtype=jnp.int32)
    inverse = jnp.zeros((blk_count,), jnp.int32).at[block_perm].set(block_ids)
    query_all = gathered.reshape(blk_count, TOK_DEV, row_width)[inverse].reshape(
        req_count, NEW, row_width
    )
    global_ids = my_index * P_DEV + jnp.arange(P_DEV, dtype=jnp.int32)
    table_ids = jnp.arange(page_table.shape[0], dtype=jnp.int32)
    match_rows = page_table[None, :] == global_ids[:, None]
    logical = jnp.sum(jnp.where(match_rows, table_ids[None, :], 0), axis=1)
    page_req = logical // MAXP
    page_pos = logical % MAXP
    page_fill = jnp.clip(cache_len[page_req] - page_pos * PAGE, 0, PAGE)
    slot_ids = jnp.arange(PAGE, dtype=jnp.int32)
    start_state = (
        jnp.zeros((req_count, NEW, head_count, HD), jnp.float32),
        jnp.full((req_count, NEW, head_count), -1e30, jnp.float32),
        jnp.zeros((req_count, NEW, head_count), jnp.float32),
    )

    def page_work(slot_index, carry_state):
        request = page_req[slot_index]
        query_rows = lax.dynamic_index_in_dim(query_all, request, 0, keepdims=False)
        key_rows = lax.dynamic_index_in_dim(key_cache, slot_index, 0, keepdims=False)
        value_rows = lax.dynamic_index_in_dim(value_cache, slot_index, 0, keepdims=False)
        visible = jnp.broadcast_to((slot_ids < page_fill[slot_index])[None, :], (NEW, PAGE))
        return absorb(
            carry_state, request, block_partial(query_rows, key_rows, value_rows, visible)
        )

    def page_step(slot_index, carry_state):
        return page_work(slot_index, carry_state)

    carry_state = lax.fori_loop(0, P_DEV, page_step, start_state)
    my_block = block_perm[my_index]
    my_request = my_block // blocks_per_req
    my_offset = my_block % blocks_per_req * TOK_DEV
    new_pos = jnp.arange(NEW, dtype=jnp.int32)[:, None]
    key_pos = my_offset + jnp.arange(TOK_DEV, dtype=jnp.int32)[None, :]
    own_rows = lax.dynamic_index_in_dim(query_all, my_request, 0, keepdims=False)
    carry_state = absorb(
        carry_state, my_request, block_partial(own_rows, new_keys, new_values, new_pos >= key_pos)
    )
    numer_all, top_all, sum_all = carry_state
    send_numer = numer_all.reshape(blk_count, TOK_DEV, row_width)[block_perm]
    send_top = top_all.reshape(blk_count, TOK_DEV, head_count)[block_perm]
    send_sum = sum_all.reshape(blk_count, TOK_DEV, head_count)[block_perm]
    recv_numer, recv_top, recv_sum = (
        lax.all_to_all(send_numer, "blk", split_axis=0, concat_axis=0, tiled=True),
        lax.all_to_all(send_top, "blk", split_axis=0, concat_axis=0, tiled=True),
        lax.all_to_all(send_sum, "blk", split_axis=0, concat_axis=0, tiled=True),
    )
    best_top = jnp.max(recv_top, axis=0)
    factor = jnp.exp(recv_top - best_top[None])
    total_sum = jnp.sum(recv_sum * factor, axis=0)
    total_numer = jnp.sum(
        recv_numer.reshape(blk_count, TOK_DEV, head_count, HD) * factor[..., None], axis=0
    )
    mixed = (total_numer / total_sum[:, :, None]).reshape(TOK_DEV, row_width).astype(jnp.bfloat16)
    head_term = jnp.dot(mixed, out_weight, preferred_element_type=jnp.float32)
    return lax.psum_scatter(head_term, "head", scatter_dimension=1, tiled=True).astype(jnp.bfloat16)


MESH = pl.DeviceIdType.MESH
Z, Y, CORES, XS = 4, 2, 2, 2
HEADS_CORE = 4
GROUP = HEADS_CORE * HD
CACHED = CORES * P_DEV * PAGE
FRESH = CORES * TOK_DEV
KEYS = CACHED + FRESH
QCHIP = CORES * TOK_DEV
QW = Y * QCHIP
VROWS = HD + 16
COLS = 1792
CHUNK = COLS // 2
WINDOW = 384
UNITS = HEADS_CORE * Z
LAG = 2
LOG2_SCALE = math.log2(math.e) / math.sqrt(HD)


def fits_fused(mesh):
    return dict(mesh.shape) == {"blk": Z * Y * CORES, "head": XS}


def fused_kernel(
    perm, q_hbm, nk_hbm, nv_hbm, kc_hbm, vc_hbm, w_hbm, out_ref,
    q_stage, nk_stage, nv_stage, k_stage, v_stage, w_all,
    q_t, k_heads, v_t, scores_a, scores_b, probs_a, probs_b, tops,
    part, part_16, part_stat, y_part, y_stat,
    z_src, z_src_stat, z_part, z_stat,
    acc, c_part, x_src, x_part, w_far, w_near, mix_src, mix_in,
    local_sem, core_send, core_recv, gz_send, gz_recv, gy_send, gy_recv,
    ry_send, ry_recv, rz_send, rz_recv, o_send, o_recv, w_send, w_recv, m_send, m_recv,
):
    me = lax.axis_index("blk")
    x = lax.axis_index("head")
    core = me % CORES
    y = (me // CORES) % Y
    z = me // (CORES * Y)
    scores, probs = (scores_a, scores_b), (probs_a, probs_b)

    def blk_of(zz, yy, cc):
        return (zz * Y + yy) * CORES + cc

    sibling = (blk_of(z, y, 1 - core), x)
    y_peer = (blk_of(z, 1 - y, core), x)
    x_peer = (me, 1 - x)
    x_sibling = (blk_of(z, y, 1 - core), 1 - x)
    last = HEADS_CORE - 1

    def z_to(d):
        return (blk_of((z + d) % Z, y, core), x)

    def remote(src, dst, send_sem, recv_sem, peer):
        return pltpu.make_async_remote_copy(
            src_ref=src, dst_ref=dst, send_sem=send_sem, recv_sem=recv_sem,
            device_id=peer, device_id_type=MESH)

    barrier = pltpu.get_barrier_semaphore()
    peers = [sibling, y_peer, x_peer, x_sibling] + [z_to(d) for d in range(1, Z)]
    for peer in peers:
        pl.semaphore_signal(barrier, inc=1, device_id=peer, device_id_type=MESH)

    mine = pl.ds(pl.multiple_of(core * GROUP, 128), GROUP)
    theirs = pl.ds(pl.multiple_of((1 - core) * GROUP, 128), GROUP)
    staged = [
        (q_hbm, q_stage), (kc_hbm, k_stage), (nk_hbm, nk_stage),
        (vc_hbm, v_stage), (nv_hbm, nv_stage),
    ]
    local_copies, core_copies = [], []
    for i, (src, dst) in enumerate(staged):
        lead = (slice(None),) * (len(src.shape) - 1)
        copy = pltpu.make_async_copy(src.at[lead + (mine,)], dst.at[core], local_sem.at[i])
        copy.start()
        local_copies.append(copy)

    pl.semaphore_wait(barrier, len(peers))
    for i, (src, dst) in enumerate(staged):
        lead = (slice(None),) * (len(src.shape) - 1)
        copy = remote(
            src.at[lead + (theirs,)], dst.at[core], core_send.at[i], core_recv.at[i], sibling)
        copy.start()
        core_copies.append(copy)
    w_copy = pltpu.make_async_copy(
        w_hbm.at[pl.ds(pl.multiple_of(core * GROUP, 128), GROUP), :], w_all, local_sem.at[5])
    w_copy.start()
    near_row = pl.multiple_of((1 - core) * GROUP + last * HD, 32)
    near_copy = pltpu.make_async_copy(
        w_hbm.at[pl.ds(near_row, HD), pl.ds(pl.multiple_of(x * COLS, 128), COLS)],
        w_near, local_sem.at[6])
    near_copy.start()
    far_copies = []
    for c in range(CORES):
        copy = remote(
            w_hbm.at[pl.ds(c * GROUP + last * HD, HD),
                     pl.ds(pl.multiple_of((1 - x) * COLS, 128), COLS)],
            w_far.at[c], w_send.at[c], w_recv.at[c], x_peer)
        copy.start()
        far_copies.append(copy)

    def arrived(i):
        local_copies[i].wait()
        core_copies[i].wait_recv()

    def gather_z(h, d):
        block = q_t.at[h, z, y]
        return remote(block, block, gz_send.at[h, d], gz_recv.at[h, d], z_to(d))

    def gather_y(h, d):
        block = q_t.at[h, (z + Z - d) % Z, y]
        return remote(block, block, gy_send.at[h, d], gy_recv.at[h, d], y_peer)

    def forward(h, d):
        gather_z(h, d).wait_recv()
        gather_y(h, d).start()

    def reduce_y(h, g):
        return (
            remote(part_16.at[h, g, 1 - y], y_part.at[h, g],
                   ry_send.at[h, g, 0], ry_recv.at[h, g, 0], y_peer),
            remote(part_stat.at[h, g, 1 - y], y_stat.at[h, g],
                   ry_send.at[h, g, 1], ry_recv.at[h, g, 1], y_peer),
        )

    def reduce_z(h, d):
        to = (z + d) % Z
        return (
            remote(z_src.at[h, to], z_part.at[h, d],
                   rz_send.at[h, d, 0], rz_recv.at[h, d, 0], z_to(d)),
            remote(z_src_stat.at[h, to], z_stat.at[h, d],
                   rz_send.at[h, d, 1], rz_recv.at[h, d, 1], z_to(d)),
        )

    arrived(0)
    q_rows = jnp.concatenate([q_stage[0], q_stage[1]], axis=0).astype(jnp.float32)
    q_cols = q_rows.T.astype(jnp.bfloat16)
    for h in range(HEADS_CORE):
        q_t[h, z, y] = q_cols[h * HD:(h + 1) * HD]

    def send_queries(h):
        for d in range(1, Z):
            gather_z(h, d).start()
        gather_y(h, 0).start()

    for h in range(HEADS_CORE):
        send_queries(h)

    v_t[:, pl.ds(HD, VROWS - HD), :] = jnp.ones((HEADS_CORE, VROWS - HD, KEYS), jnp.bfloat16)
    acc[...] = jnp.zeros(acc.shape, jnp.float32)

    def head_window(h):
        start = jnp.minimum(h * HD // 128 * 128, GROUP - WINDOW)
        return pl.ds(pl.multiple_of(start, 128), WINDOW), h * HD - start

    def prepare_keys(h):
        window, offset = head_window(h)
        pick = jnp.where(
            lax.broadcasted_iota(jnp.int32, (WINDOW, HD), 0)
            == lax.broadcasted_iota(jnp.int32, (WINDOW, HD), 1) + offset, 1.0, 0.0
        ).astype(jnp.bfloat16)

        def place(rows, at, count):
            k_heads[h, pl.ds(at, count), :] = jnp.dot(
                rows, pick, preferred_element_type=jnp.float32).astype(jnp.bfloat16)

        for c in range(CORES):
            for page in range(0, P_DEV, 2):
                rows = k_stage[c, pl.ds(page, 2), :, window].reshape(2 * PAGE, WINDOW)
                place(rows, (c * P_DEV + page) * PAGE, 2 * PAGE)
            place(nk_stage[c, :, window], CACHED + c * TOK_DEV, TOK_DEV)

    def prepare_values(h):
        window, offset = head_window(h)
        pick = jnp.where(
            lax.broadcasted_iota(jnp.int32, (HD, WINDOW), 1)
            == lax.broadcasted_iota(jnp.int32, (HD, WINDOW), 0) + offset, 1.0, 0.0
        ).astype(jnp.bfloat16)

        def place(rows, at, count):
            v_t[h, pl.ds(0, HD), pl.ds(at, count)] = lax.dot_general(
                pick, rows, (((1,), (1,)), ((), ())), preferred_element_type=jnp.float32
            ).astype(jnp.bfloat16)

        for c in range(CORES):
            for page in range(0, P_DEV, 2):
                rows = v_stage[c, pl.ds(page, 2), :, window].reshape(2 * PAGE, WINDOW)
                place(rows, (c * P_DEV + page) * PAGE, 2 * PAGE)
        place(jnp.concatenate([nv_stage[c, :, window] for c in range(CORES)], axis=0), CACHED, FRESH)

    row = lax.broadcasted_iota(jnp.int32, (FRESH, QW), 0)
    lane = lax.broadcasted_iota(jnp.int32, (FRESH, QW), 1)
    tile_row = lax.broadcasted_iota(jnp.int32, (2, QCHIP), 0)

    def unit_of(u):
        h, t = u // Z, u % Z
        return h, (t + h // (HEADS_CORE - 1)) % Z

    def score_tiles(u, par):
        h, k = unit_of(u)
        g = (z + k) % Z
        queries = jnp.concatenate([q_t[h, g, 0], q_t[h, g, 1]], axis=1)
        top = [None]

        def rows_from(at):
            tile = jnp.dot(
                k_heads[h, pl.ds(at, KEYS // 2), :], queries, preferred_element_type=jnp.float32)
            if at > 0:
                key_pos = jnp.where(
                    row < TOK_DEV, perm[blk_of(z, y, 0)], perm[blk_of(z, y, 1)]
                ) * TOK_DEV + row % TOK_DEV
                query_blk = jnp.zeros((FRESH, QW), jnp.int32)
                for j in range(Y * CORES):
                    query_blk = jnp.where(lane // TOK_DEV == j, perm[g * Y * CORES + j], query_blk)
                seen = query_blk * TOK_DEV + lane % TOK_DEV >= key_pos
                tile = jnp.concatenate(
                    [tile[:CACHED - at], jnp.where(seen, tile[CACHED - at:], -1e30)], axis=0)
            scores[par][pl.ds(at, KEYS // 2), :] = tile
            tile_top = jnp.max(tile.reshape(KEYS // 16, 8, QW), axis=0)
            top[0] = tile_top if top[0] is None else jnp.maximum(top[0], tile_top)
            if at > 0:
                tops[par] = jnp.broadcast_to(
                    jnp.max(top[0], axis=0, keepdims=True) * LOG2_SCALE, (8, QW))

        steps = [lambda: None] * 9
        steps[1] = lambda: rows_from(0)
        steps[5] = lambda: rows_from(KEYS // 2)
        return steps

    def weight_tiles(par):
        top = tops[par][0:1]
        tops[2 + par] = tops[par]

        def weigh(at, count):
            tile = scores[par][pl.ds(at, count), :]
            probs[par][pl.ds(at, count), :] = jnp.exp2(tile * LOG2_SCALE - top).astype(jnp.bfloat16)

        spans = [(i * 256, 256) for i in range(CACHED // 256)] + [(CACHED, FRESH)]
        return [lambda s=s: weigh(*s) for s in spans]

    def value_tiles(u, par, numer):
        h, _ = unit_of(u)

        def add(at, count):
            term = jnp.dot(
                v_t[h, :, pl.ds(at, count)], probs[par][pl.ds(at, count), :],
                preferred_element_type=jnp.float32)
            numer[0] = term if numer[0] is None else numer[0] + term

        def nothing():
            pass

        steps = [nothing] * 9
        steps[0] = lambda: add(0, KEYS)
        return steps

    def merge(u):
        h, k = unit_of(u)
        g = (z + k) % Z
        for copy in reduce_y(h, g):
            copy.wait_recv()
        own, other = part_stat[h, g, y], y_stat[h, g]
        top = jnp.maximum(own[0:1], other[0:1])
        own_factor, other_factor = jnp.exp2(own[0:1] - top), jnp.exp2(other[0:1] - top)
        total = own[1:2] * own_factor + other[1:2] * other_factor
        numer = part[h, g, y] * own_factor + y_part[h, g].astype(jnp.float32) * other_factor
        z_src[h, g] = numer.astype(jnp.bfloat16)
        z_src_stat[h, g] = jnp.where(tile_row == 0, top, total)

        @pl.when(k > 0)
        def _():
            for copy in reduce_z(h, k):
                copy.start()

    def mix(h):
        for d in range(1, Z):
            for copy in reduce_z(h, d):
                copy.wait_recv()
        stats = [z_src_stat[h, z]] + [z_stat[h, d] for d in range(1, Z)]
        numers = [z_src[h, z]] + [z_part[h, d] for d in range(1, Z)]
        top = stats[0][0:1]
        for stat in stats[1:]:
            top = jnp.maximum(top, stat[0:1])
        total = jnp.zeros((1, QCHIP), jnp.float32)
        numer = jnp.zeros((HD, QCHIP), jnp.float32)
        for stat, term in zip(stats, numers):
            factor = jnp.exp2(stat[0:1] - top)
            total = total + stat[1:2] * factor
            numer = numer + term.astype(jnp.float32) * factor
        return (numer / total).T.astype(jnp.bfloat16)

    def finish(h, send=None):
        mixed = mix(h)
        w_rows = pl.ds(pl.multiple_of(h * HD, 32), HD)
        for place, half in enumerate((1 - x, x)):
            for part_index in range(2):
                for at, count in ((0, 512), (512, 384)):
                    w_cols = pl.ds(
                        pl.multiple_of(half * COLS + part_index * CHUNK + at, 128), count)
                    term = jnp.dot(mixed, w_all[w_rows, w_cols], preferred_element_type=jnp.float32)
                    for c in range(CORES):
                        acc[half, part_index, c, :, pl.ds(at, count)] += (
                            term[c * TOK_DEV:(c + 1) * TOK_DEV])
                if send is not None:
                    send(place, half, part_index)

    def step(u, par, score, weigh, value):
        lists = []
        numer = [None]
        old_top = tops[2 + par][0:1] if value else None
        if score:
            h, k = unit_of(u)
            d = (Z - k) % Z
            gather_y(h, d).wait_recv()

            @pl.when((k > 0) & (h < HEADS_CORE - 1))
            def _():
                forward(h + 1, d)

        if value:
            lists.append(value_tiles(u - 2, par, numer))
        if weigh:
            lists.append(weight_tiles(1 - par))
        if score:
            lists.append(score_tiles(u, par))
        for group in zip(*lists):
            for work in group:
                work()
        if value:
            h, k = unit_of(u - 2)
            g = (z + k) % Z
            for j in range(Y):
                cols = slice(j * QCHIP, (j + 1) * QCHIP)
                part[h, g, j] = numer[0][:HD, cols]
                part_16[h, g, j] = numer[0][:HD, cols].astype(jnp.bfloat16)
                part_stat[h, g, j] = jnp.where(
                    tile_row == 0, old_top[:, cols], numer[0][HD:HD + 1, cols])
            for copy in reduce_y(h, g):
                copy.start()

    def beside(u):
        @pl.when((u % Z == 2) & (u < UNITS - Z))
        def _():
            prepare_keys(u // Z + 1)
            prepare_values(u // Z + 1)

        @pl.when(u >= 2 + LAG)
        def _():
            merge(u - 2 - LAG)

        @pl.when((u >= 10) & (u % Z == 2))
        def _():
            finish((u - 10) // Z)

    arrived(1)
    arrived(2)
    prepare_keys(0)
    for d in range(1, Z):
        forward(0, d)
    step(0, 0, True, False, False)
    step(1, 1, True, True, False)
    arrived(3)
    arrived(4)
    prepare_values(0)
    w_copy.wait()

    @pl.loop(1, UNITS // 2)
    def _(pair):
        for par in range(2):
            step(2 * pair + par, par, True, True, True)
            beside(2 * pair + par)

    step(UNITS, 0, False, True, True)
    merge(UNITS - 2 - LAG)
    step(UNITS + 1, 1, False, False, True)
    merge(UNITS - 1 - LAG)
    core_out = {}

    def send_core(place, half, part_index):
        i = place * 2 + part_index
        core_out[i] = remote(
            acc.at[half, part_index, 1 - core], c_part.at[place, part_index],
            o_send.at[i], o_recv.at[i], sibling)
        core_out[i].start()

    finish(last - 1, send_core)
    merge(UNITS - 2)
    across = []
    for i in range(2):
        core_out[i].wait_recv()
        x_src[i] = (acc[1 - x, i, core] + c_part[0, i]).astype(jnp.bfloat16)
        copy = remote(x_src.at[i], x_part.at[i], o_send.at[4 + i], o_recv.at[4 + i], x_peer)
        copy.start()
        across.append(copy)
    merge(UNITS - 1)
    for i in range(2):
        core_out[2 + i].wait_recv()
        c_part[1, i] = acc[x, i, core] + c_part[1, i]
    near_copy.wait()
    for copy in far_copies:
        copy.wait_recv()

    mixed = mix(last)
    for c in range(CORES):
        mix_src[c] = jnp.concatenate(
            [mixed[c * TOK_DEV:(c + 1) * TOK_DEV], jnp.zeros((TOK_DEV, 256 - HD), jnp.bfloat16)],
            axis=1)
    mix_copies = []
    for i, (rows, peer) in enumerate(((core, x_peer), (1 - core, x_sibling), (1 - core, sibling))):
        copy = remote(mix_src.at[rows], mix_in.at[i], m_send.at[i], m_recv.at[i], peer)
        copy.start()
        mix_copies.append(copy)

    spans = ((0, 512), (512, 384), (CHUNK, 512), (CHUNK + 512, 384))

    def add_rows(rows, weight_of):
        for at, count in spans:
            i, inner = at // CHUNK, at % CHUNK
            c_part[1, i, :, pl.ds(inner, count)] += jnp.dot(
                rows, weight_of(at, count), preferred_element_type=jnp.float32)

    def own_weight(at, count):
        cols = pl.ds(pl.multiple_of(x * COLS + at, 128), count)
        return w_all[pl.ds(last * HD, HD), cols]

    add_rows(mix_src[core][:, :HD], own_weight)
    for i in range(2):
        across[i].wait_recv()
        c_part[1, i] += x_part[i].astype(jnp.float32)
    mix_copies[2].wait_recv()
    add_rows(mix_in[2][:, :HD], lambda at, count: w_near[:, pl.ds(at, count)])
    mix_copies[0].wait_recv()
    mix_copies[1].wait_recv()
    for at, count in spans:
        i, inner = at // CHUNK, at % CHUNK
        same = jnp.dot(
            mix_in[0][:, :HD], w_far[core, :, pl.ds(at, count)],
            preferred_element_type=jnp.float32)
        other = jnp.dot(
            mix_in[1][:, :HD], w_far[1 - core, :, pl.ds(at, count)],
            preferred_element_type=jnp.float32)
        out_ref[:, pl.ds(at, count)] = (
            c_part[1, i, :, pl.ds(inner, count)] + same + other).astype(jnp.bfloat16)

    for copy in far_copies + mix_copies:
        copy.wait_send()
    for copy in core_copies + list(core_out.values()) + across:
        copy.wait_send()

    @pl.loop(0, HEADS_CORE)
    def _(h):
        for d in range(Z):
            gather_y(h, d).wait_send()
            for copy in reduce_y(h, d):
                copy.wait_send()
            if d > 0:
                gather_z(h, d).wait_send()
                for copy in reduce_z(h, d):
                    copy.wait_send()


def fused_shards(
    queries, new_keys, new_values, key_cache, value_cache, out_weight,
    cache_len, page_table, block_perm,
):
    bf16, f32 = jnp.bfloat16, jnp.float32
    vmem, dma = pltpu.VMEM, pltpu.SemaphoreType.DMA
    hc = HEADS_CORE
    block = (HD, QCHIP)
    stat = (2, QCHIP)
    scratch = [
        vmem((CORES, TOK_DEV, GROUP), bf16),
        vmem((CORES, TOK_DEV, GROUP), bf16),
        vmem((CORES, TOK_DEV, GROUP), bf16),
        vmem((CORES, P_DEV, PAGE, GROUP), bf16),
        vmem((CORES, P_DEV, PAGE, GROUP), bf16),
        vmem((GROUP, XS * COLS), bf16),
        vmem((hc, Z, Y) + block, bf16),
        vmem((hc, KEYS, HD), bf16),
        vmem((hc, VROWS, KEYS), bf16),
        vmem((KEYS, QW), f32),
        vmem((KEYS, QW), f32),
        vmem((KEYS, QW), bf16),
        vmem((KEYS, QW), bf16),
        vmem((4, 8, QW), f32),
        vmem((hc, Z, Y) + block, f32),
        vmem((hc, Z, Y) + block, bf16),
        vmem((hc, Z, Y) + stat, f32),
        vmem((hc, Z) + block, bf16),
        vmem((hc, Z) + stat, f32),
        vmem((hc, Z) + block, bf16),
        vmem((hc, Z) + stat, f32),
        vmem((hc, Z) + block, bf16),
        vmem((hc, Z) + stat, f32),
        vmem((XS, 2, CORES, TOK_DEV, CHUNK), f32),
        vmem((2, 2, TOK_DEV, CHUNK), f32),
        vmem((2, TOK_DEV, CHUNK), bf16),
        vmem((2, TOK_DEV, CHUNK), bf16),
        vmem((CORES, HD, COLS), bf16),
        vmem((HD, COLS), bf16),
        vmem((CORES, TOK_DEV, 256), bf16),
        vmem((3, TOK_DEV, 256), bf16),
        dma((7,)), dma((5,)), dma((5,)),
        dma((hc, Z)), dma((hc, Z)), dma((hc, Z)), dma((hc, Z)),
        dma((hc, Z, 2)), dma((hc, Z, 2)), dma((hc, Z, 2)), dma((hc, Z, 2)),
        dma((6,)), dma((6,)), dma((2,)), dma((2,)), dma((3,)), dma((3,)),
    ]
    flops = 4 * hc * Z * QW * KEYS * HD + 2 * QCHIP * GROUP * XS * COLS
    return pl.pallas_call(
        fused_kernel,
        out_shape=jax.ShapeDtypeStruct((TOK_DEV, COLS), bf16),
        in_specs=[pl.BlockSpec(memory_space=pltpu.SMEM)] + [pl.BlockSpec(memory_space=pl.ANY)] * 6,
        out_specs=pl.BlockSpec(memory_space=pltpu.VMEM),
        scratch_shapes=scratch,
        compiler_params=pltpu.CompilerParams(
            collective_id=0, has_side_effects=True, vmem_limit_bytes=56 * 1024 * 1024),
        cost_estimate=pl.CostEstimate(
            flops=flops, bytes_accessed=14 * 1024 * 1024, transcendentals=hc * Z * QW * KEYS),
    )(block_perm, queries, new_keys, new_values, key_cache, value_cache, out_weight)


def solution(mesh):
    in_specs = (
        P("blk", "head"),
        P("blk", "head"),
        P("blk", "head"),
        P("blk", None, "head"),
        P("blk", None, "head"),
        P("head", None),
        P(),
        P(),
        P(),
    )
    out_specs = P("blk", "head")
    local = fused_shards if fits_fused(mesh) else shards
    return jax.shard_map(local, mesh=mesh, in_specs=in_specs, out_specs=out_specs, check_vma=False)
```
